256 devices in a mesh: expert: 16 (over x_hi, y, core), dp: 16 (over x_lo, z).
Axes of the slice: x: 4 (x_hi: 2, x_lo: 2; x = x_hi * 2 + x_lo), y: 4, z: 8, core: 2. Of those that a mesh axis runs over, the one named last changes fastest.
Arguments:
- cotangent: bfloat16 [32768, 2048], P(('expert', 'dp')), may hold values from -6 to 6
- hidden: bfloat16 [32768, 7168], P(('expert', 'dp')), may hold values from -0.1796875 to 0.1796875
- codes: bfloat16 [16, 7168, 1024], P('expert', 'dp'), may hold values from -0.125 to 0.125
- scales: float32 [16, 7168], P('expert', 'dp'), may hold values from 0.3 to 3
- counts: int32 [256, 8], replicated, may hold values from 0 to 24, as said below
Outputs:
- d_hidden: bfloat16 [32768, 7168], P(('expert', 'dp'))
- weight_grad: float32 [16, 7168, 1024], P('expert', 'dp')
The draws below stay inside these ranges and needn't reach their ends.
Inputs may be any that keep to these rules, and one draw needn't show every extreme that they name: Row p of counts is device p's split of its 128 rows over the experts, devices numbered with the expert index first; a device's rows are grouped by expert in increasing order. Each row sums to 128 and has an entry equal to 24. In every draw all devices of one pair of neighbouring expert indices give their 24 rows to the same expert.
All inputs are finite; a program needn't handle non-finite values.
Results may differ from the reference program's by a relative error of at most 0.001.
Values may be sent and summed in bfloat16 or wider, within the bound.
No kernel may reach another device: no remote copies, remote signals or barrier semaphores. Data moves between devices by JAX's collectives and lax.ppermute only.
A program may use at most 192 MiB of HBM per device.

```python
import math
import jax
import jax.numpy as jnp
from jax import lax

D = 2048
FF = 7168
ROWS = 128
EXPERTS = 8
MOST = 24
TOKENS = 32768
N_EXPERT = 16


def draw_counts(key, part):
    key = jax.random.fold_in(key, 7)
    device_count = TOKENS // ROWS
    expert_count = EXPERTS
    subkeys = jax.random.split(key, 4)
    device_ids = jnp.arange(device_count, dtype=jnp.int32)
    group_ids = device_ids // (device_count // expert_count)
    device_hot = jax.random.randint(subkeys[0], (device_count,), 0, expert_count)
    shared_hot = jax.random.randint(subkeys[1], (), 0, expert_count)
    chosen_group = jax.random.randint(subkeys[2], (), 0, expert_count)
    hot_expert = jnp.where(group_ids == chosen_group, shared_hot, device_hot).astype(jnp.int32)
    remaining = ROWS - MOST
    other_total = expert_count - 1
    other_ids = jnp.arange(other_total, dtype=jnp.int32)
    base_loads = remaining // other_total + (other_ids < remaining % other_total).astype(jnp.int32)
    other_loads = jnp.broadcast_to(base_loads[None, :], (device_count, other_total)).astype(jnp.int32)
    for round_index in range(6):
        round_key = jax.random.fold_in(subkeys[3], round_index)
        key_source, key_target, key_amount = jax.random.split(round_key, 3)
        source_rank = jax.random.randint(key_source, (device_count,), 0, other_total)
        target_rank = (source_rank + 1 + jax.random.randint(key_target, (device_count,), 0, other_total - 1)) % other_total
        wanted = jax.random.randint(key_amount, (device_count,), 0, MOST + 1)
        source_load = jnp.take_along_axis(other_loads, source_rank[:, None], 1)[:, 0]
        target_load = jnp.take_along_axis(other_loads, target_rank[:, None], 1)[:, 0]
        move_size = jnp.minimum(jnp.minimum(wanted, source_load), MOST - target_load)
        at_source = (other_ids[None, :] == source_rank[:, None]).astype(jnp.int32)
        at_target = (other_ids[None, :] == target_rank[:, None]).astype(jnp.int32)
        other_loads = other_loads - move_size[:, None] * at_source + move_size[:, None] * at_target
    other_rank = (jnp.arange(expert_count, dtype=jnp.int32)[None, :] - hot_expert[:, None] - 1) % expert_count
    picked_loads = jnp.take_along_axis(other_loads, jnp.minimum(other_rank, other_total - 1), 1)
    return jnp.where(other_rank == other_total, MOST, picked_loads).astype(jnp.int32)


def levels(key, dims, shards, smallest, largest):
    level, own = 1.0, jax.random.fold_in(key, 6)
    for dim, blocks in shards:
        heights = jnp.exp(jax.random.uniform(jax.random.fold_in(own, dim), (blocks,), jnp.float32, smallest / len(shards), largest / len(shards)))
        level = level * jnp.repeat(heights, dims[dim] // blocks).reshape([-1 if axis == dim else 1 for axis in range(len(dims))])
    return level


def gaussian(rng, dims, scale, limit, cuts=(), held_as=jnp.bfloat16):
    array = scale * jax.random.normal(rng, dims, jnp.float32)
    if cuts:
        array = array * levels(rng, dims, cuts, -0.22, 0.18)
    return jnp.clip(array, -limit, limit).astype(held_as)


def setup_inputs(seed: int = 0) -> dict:
    seeds = jax.random.split(jax.random.key(seed), 6)
    return {
        "cotangent": gaussian(seeds[0], (TOKENS, D), 1.0, 6.0, ((0, 256),)),
        "hidden": gaussian(seeds[1], (TOKENS, FF), 0.03, 0.1796875, ((0, 256),)),
        "codes": gaussian(seeds[2], (N_EXPERT, FF, D // 2), D ** -0.5, 0.125, ((0, 16), (1, 16))),
        "scales": jnp.clip(jnp.exp(math.log(3.0) - 2.3025851 * jax.random.uniform(seeds[3], (N_EXPERT, FF), jnp.float32) ** levels(seeds[3], (N_EXPERT, FF), ((0, 16), (1, 16)), -0.2, 0.2)), 0.3, 3.0),
        "counts": draw_counts(jax.random.fold_in(seeds[5], 71), 0),
    }


def reference(cotangent, hidden, codes, scales, counts):
    device_count = counts.shape[0]
    half_cols = D // 2
    row_starts = (jnp.cumsum(counts, axis=1).astype(jnp.int32) - counts).astype(jnp.int32)
    slot_range = jnp.arange(MOST, dtype=jnp.int32)
    device_base = (jnp.arange(device_count, dtype=jnp.int32) * ROWS)[:, None]

    def one_expert(running_sum, expert):
        chosen_count = lax.dynamic_index_in_dim(counts, expert, 1, keepdims=False)
        chosen_start = lax.dynamic_index_in_dim(row_starts, expert, 1, keepdims=False)
        slot_valid = (slot_range[None, :] < chosen_count[:, None]).reshape(-1)
        slot_index = (device_base + jnp.minimum(chosen_start[:, None] + slot_range[None, :], ROWS - 1)).reshape(-1).astype(jnp.int32)
        values_tile = jnp.where(slot_valid[:, None], cotangent[slot_index], jnp.zeros((), cotangent.dtype))
        hidden_tile = jnp.where(slot_valid[:, None], hidden[slot_index], jnp.zeros((), hidden.dtype))
        codes_low = lax.dynamic_index_in_dim(codes, 2 * expert, 0, keepdims=False)
        codes_high = lax.dynamic_index_in_dim(codes, 2 * expert + 1, 0, keepdims=False)
        scale_low = lax.dynamic_index_in_dim(scales, 2 * expert, 0, keepdims=False)
        scale_high = lax.dynamic_index_in_dim(scales, 2 * expert + 1, 0, keepdims=False)
        partial_low = jnp.dot(values_tile[:, :half_cols], codes_low.T, preferred_element_type=jnp.float32) * scale_low[None, :]
        partial_high = jnp.dot(values_tile[:, half_cols:], codes_high.T, preferred_element_type=jnp.float32) * scale_high[None, :]
        partial_value = partial_low + partial_high
        running_sum = running_sum.at[slot_index].add(jnp.where(slot_valid[:, None], partial_value, jnp.zeros((), partial_value.dtype)))
        weight_term = jnp.dot(hidden_tile.T, values_tile, preferred_element_type=jnp.float32)
        return running_sum, weight_term

    running_sum, weight_terms = lax.scan(one_expert, jnp.zeros((TOKENS, FF), jnp.float32), jnp.arange(EXPERTS, dtype=jnp.int32))
    d_hidden = running_sum.astype(jnp.bfloat16)
    weight_grad = weight_terms.reshape(EXPERTS, FF, 2, half_cols).transpose(0, 2, 1, 3).reshape(2 * EXPERTS, FF, half_cols)
    return d_hidden, weight_grad
```

```python
import jax
import jax.numpy as jnp
from jax import lax
from jax.sharding import Mesh, PartitionSpec as P

PLACES = ("xh", "y")
SWAP = [(0, 1), (1, 0)]


def slot_hot(row_counts, slots, rows):
    starts = jnp.cumsum(row_counts, axis=-1) - row_counts
    slot = jnp.arange(slots, dtype=jnp.int32)
    source = jnp.where(slot < row_counts[..., None], starts[..., None] + slot, -1)
    return (source[..., None] == jnp.arange(rows, dtype=jnp.int32)).astype(jnp.bfloat16)


def shards(cotangent, hidden, codes, scales, counts):
    rows, cols = cotangent.shape
    width = hidden.shape[1]
    half = cols // 2
    share = codes.shape[1]
    places = lax.axis_size(PLACES)
    depth = lax.axis_size("z")
    experts = counts.shape[1]
    slots = 3 * rows // (2 * experts)
    wide = 2 * share
    place, core = lax.axis_index(PLACES), lax.axis_index("c")
    side, level = lax.axis_index("xl"), lax.axis_index("z")
    table = counts.reshape(places, 2, 2, depth, experts)
    line_counts = lax.dynamic_slice(
        table, (place, core, side, 0, 0), (1, 1, 1, depth, experts)
    ).reshape(depth, experts)
    own_counts = lax.dynamic_slice_in_dim(line_counts, level, 1, 0)[0]
    own_hot = slot_hot(own_counts, slots, rows).reshape(experts * slots, rows)
    line_hot = slot_hot(line_counts, slots, rows)

    packed = jnp.stack(
        [
            jnp.dot(own_hot, cotangent[:, c * half : (c + 1) * half],
                    preferred_element_type=jnp.float32).astype(jnp.bfloat16)
            for c in range(2)
        ]
    ).reshape(2 * experts, slots, half)
    arrived = lax.all_to_all(packed, ("c",) + PLACES, 0, 0).reshape(2, places * slots, half)
    mate_rows = lax.dynamic_index_in_dim(arrived, 1 - core, 0, keepdims=False)
    own_rows = lax.dynamic_index_in_dim(arrived, core, 0, keepdims=False)
    mate_all = lax.all_gather(mate_rows, "z", axis=0, tiled=True)
    own_all = lax.all_gather(own_rows, "z", axis=0, tiled=True)

    other_codes, other_scales = lax.ppermute((codes[0], scales[0]), "xl", SWAP)
    first = side == 0
    both_codes = jnp.where(first, jnp.stack([codes[0], other_codes]),
                           jnp.stack([other_codes, codes[0]])).reshape(wide, half)
    both_scales = jnp.where(first, jnp.stack([scales[0], other_scales]),
                            jnp.stack([other_scales, scales[0]])).reshape(wide)

    by_level = hidden.reshape(rows, 2, depth, share).transpose(2, 0, 1, 3).reshape(depth, rows, wide)
    line_hidden = lax.all_to_all(by_level, "z", 0, 0)
    hidden_slots = jnp.einsum("zesr,zrw->ezsw", line_hot, line_hidden,
                              preferred_element_type=jnp.float32).astype(jnp.bfloat16)
    own_hidden = lax.all_to_all(hidden_slots, PLACES, 0, 0)
    own_hidden = own_hidden.transpose(1, 0, 2, 3).reshape(depth * places * slots, wide)
    mate_hidden = lax.ppermute(own_hidden, "c", SWAP)

    def partial(values):
        return lax.dot_general(values, both_codes, (((1,), (1,)), ((), ())),
                               preferred_element_type=jnp.float32) * both_scales[None, :]

    def weight(units, values):
        return lax.dot_general(units, values, (((0,), (0,)), ((), ())),
                               preferred_element_type=jnp.float32)

    mate_partial = lax.ppermute(partial(mate_all), "c", SWAP)
    joined = (partial(own_all) + mate_partial).astype(jnp.bfloat16)
    joined = joined.reshape(depth, places, slots, wide).transpose(1, 0, 2, 3)
    back = lax.all_to_all(joined, PLACES, 0, 0)
    line_back = jnp.einsum("zesr,ezsw->zrw", line_hot, back,
                           preferred_element_type=jnp.float32).astype(jnp.bfloat16)
    home = lax.all_to_all(line_back, "z", 0, 0)
    d_hidden = home.reshape(depth, rows, 2, share).transpose(1, 2, 0, 3).reshape(rows, width)

    sums = (weight(mate_hidden, mate_all) + weight(own_hidden, own_all)).reshape(2, share, half)
    gone = lax.dynamic_index_in_dim(sums, 1 - side, 0, keepdims=False)
    kept = lax.dynamic_index_in_dim(sums, side, 0, keepdims=False)
    weight_grad = kept + lax.ppermute(gone, "xl", SWAP)
    return d_hidden, weight_grad[None]


def solution(mesh):
    lanes, lines = mesh.devices.shape
    fine = Mesh(mesh.devices.reshape(2, lanes // 4, 2, 2, lines // 2), ("xh", "y", "c", "xl", "z"))
    expert, dp = ("xh", "y", "c"), ("xl", "z")
    in_specs = (P(expert + dp, None), P(expert + dp, None), P(expert, dp, None), P(expert, dp), P())
    out_specs = (P(expert + dp, None), P(expert, dp, None))
    return jax.shard_map(shards, mesh=fine, in_specs=in_specs, out_specs=out_specs, check_vma=False)
```

```python
import jax
import jax.numpy as jnp
from jax import lax
from jax.experimental import pallas as pl
from jax.experimental.pallas import tpu as pltpu
from jax.sharding import Mesh, PartitionSpec as P

PLACES = ("xh", "y")
SWAP = [(0, 1), (1, 0)]


def slot_hot(row_counts, slots, rows):
    starts = jnp.cumsum(row_counts, axis=-1) - row_counts
    slot = jnp.arange(slots, dtype=jnp.int32)
    source = jnp.where(slot < row_counts[..., None], starts[..., None] + slot, -1)
    return (source[..., None] == jnp.arange(rows, dtype=jnp.int32)).astype(jnp.bfloat16)


def distances(depth):
    near = [0]
    for k in range(1, depth // 2):
        near += [-k, k]
    return near + [depth // 2]


def far_first(depth):
    order = distances(depth)[::-1]
    return [order[:3], order[3:]]


def after(value, *others):
    return lax.optimization_barrier((value,) + others)[0]


def along_z(value, by):
    depth = lax.axis_size("z")
    return lax.ppermute(value, "z", [(i, (i + by) % depth) for i in range(depth)])


def split_kernel(level_ref, hidden_ref, *refs):
    outs, held = refs[:-1], refs[-1]
    depth, _, wide = held.shape
    share = wide // 2
    for z in range(depth):
        low = hidden_ref[:, z * share : (z + 1) * share]
        high = hidden_ref[:, (depth + z) * share : (depth + z + 1) * share]
        held[z] = jnp.concatenate([low, high], axis=1)
    for out, by in zip(outs, distances(depth)):
        out[...] = held[lax.rem(level_ref[0] + (by + depth), depth)]


def split_levels(hidden, level, depth):
    rows, width = hidden.shape
    block = (rows, width // depth)
    whole = pl.BlockSpec(memory_space=pltpu.VMEM)
    return pl.pallas_call(
        split_kernel,
        out_shape=[jax.ShapeDtypeStruct(block, hidden.dtype)] * depth,
        in_specs=[pl.BlockSpec(memory_space=pltpu.SMEM), whole],
        out_specs=[whole] * depth,
        scratch_shapes=[pltpu.VMEM((depth,) + block, hidden.dtype)],
        compiler_params=pltpu.CompilerParams(vmem_limit_bytes=32 << 20),
        cost_estimate=pl.CostEstimate(flops=0, bytes_accessed=4 * rows * width, transcendentals=0),
    )(level, hidden)


def join_kernel(level_ref, *refs):
    parts, out_ref, held = refs[:-2], refs[-2], refs[-1]
    depth, _, wide = held.shape
    share = wide // 2
    for part, by in zip(parts, distances(depth)):
        held[lax.rem(level_ref[0] + (by + depth), depth)] = part[...]
    for z in range(0, depth, 2):
        for s in range(2):
            pair = [held[z + i, :, s * share : (s + 1) * share] for i in range(2)]
            out_ref[:, (s * depth + z) * share : (s * depth + z + 2) * share] = (
                jnp.concatenate(pair, axis=1)
            )


def join_levels(parts, level):
    depth = len(parts)
    rows, wide = parts[0].shape
    whole = pl.BlockSpec(memory_space=pltpu.VMEM)
    return pl.pallas_call(
        join_kernel,
        out_shape=jax.ShapeDtypeStruct((rows, depth * wide), parts[0].dtype),
        in_specs=[pl.BlockSpec(memory_space=pltpu.SMEM)] + [whole] * depth,
        out_specs=whole,
        scratch_shapes=[pltpu.VMEM((depth, rows, wide), parts[0].dtype)],
        compiler_params=pltpu.CompilerParams(vmem_limit_bytes=32 << 20),
        cost_estimate=pl.CostEstimate(
            flops=0, bytes_accessed=4 * rows * depth * wide, transcendentals=0
        ),
    )(level, *parts)


def mate_kernel(place_ref, core_ref, rows_ref, codes_ref, scales_ref, out_ref):
    out_ref[0] = scales_ref[...] * jnp.dot(
        rows_ref[0, 0], codes_ref[...], preferred_element_type=jnp.float32
    )


def own_kernel(place_ref, core_ref, rows_ref, codes_ref, scales_ref, mate_ref, out_ref):
    total = mate_ref[0] + scales_ref[...] * jnp.dot(
        rows_ref[0, 0], codes_ref[...], preferred_element_type=jnp.float32
    )
    places, _, slots, wide = out_ref.shape
    out_ref[:, 0] = total.reshape(places, slots, wide).astype(out_ref.dtype)


def partials(where, core, values, codes, scales, mate=None, places=None):
    steps = where.shape[0]
    _, _, rows, half = values.shape
    wide = codes.shape[1]
    flip = 1 if mate is None else 0
    f32 = jax.ShapeDtypeStruct((steps, rows, wide), jnp.float32)
    in_specs = [
        pl.BlockSpec((1, 1, rows, half), lambda j, w, c: (w[j], c[0] ^ flip, 0, 0)),
        pl.BlockSpec((half, wide), lambda j, w, c: (0, 0)),
        pl.BlockSpec((1, wide), lambda j, w, c: (0, 0)),
    ]
    row_spec = pl.BlockSpec((1, rows, wide), lambda j, w, c: (j, 0, 0))
    if mate is None:
        kernel, out_shape, out_spec, extra = mate_kernel, f32, row_spec, ()
    else:
        slots = rows // places
        kernel, extra = own_kernel, (mate,)
        in_specs.append(row_spec)
        out_shape = jax.ShapeDtypeStruct((places, steps, slots, wide), jnp.bfloat16)
        out_spec = pl.BlockSpec((places, 1, slots, wide), lambda j, w, c: (0, j, 0, 0))
    return pl.pallas_call(
        kernel,
        out_shape=out_shape,
        grid_spec=pltpu.PrefetchScalarGridSpec(
            num_scalar_prefetch=2, grid=(steps,), in_specs=in_specs, out_specs=out_spec
        ),
        compiler_params=pltpu.CompilerParams(vmem_limit_bytes=32 << 20),
        cost_estimate=pl.CostEstimate(
            flops=2 * steps * rows * half * wide,
            bytes_accessed=steps * rows * (2 * half + 8 * wide),
            transcendentals=0,
        ),
    )(where, core, values, codes, scales, *extra)


def order_kernel(where_ref, core_ref, own_ref, mate_ref, out_ref):
    me = core_ref[0]
    out_ref[0, me] = own_ref[:, 0]
    out_ref[0, 1 - me] = mate_ref[:, 0]


def order_hidden(where, core, own, mate):
    places, depth, slots, wide = own.shape
    in_spec = pl.BlockSpec((places, 1, slots, wide), lambda j, w, c: (0, j, 0, 0))
    return pl.pallas_call(
        order_kernel,
        out_shape=jax.ShapeDtypeStruct((depth, 2, places, slots, wide), own.dtype),
        grid_spec=pltpu.PrefetchScalarGridSpec(
            num_scalar_prefetch=2,
            grid=(depth,),
            in_specs=[in_spec, in_spec],
            out_specs=pl.BlockSpec((1, 2, places, slots, wide), lambda j, w, c: (w[j], 0, 0, 0, 0)),
        ),
        compiler_params=pltpu.CompilerParams(vmem_limit_bytes=32 << 20),
        cost_estimate=pl.CostEstimate(
            flops=0, bytes_accessed=8 * places * depth * slots * wide, transcendentals=0
        ),
    )(where, core, own, mate)


def shards(cotangent, hidden, codes, scales, counts):
    rows, cols = cotangent.shape
    half = cols // 2
    share = codes.shape[1]
    places = lax.axis_size(PLACES)
    depth = lax.axis_size("z")
    experts = counts.shape[1]
    slots = 3 * rows // (2 * experts)
    wide = 2 * share
    order = distances(depth)
    place, core = lax.axis_index(PLACES), lax.axis_index("c")
    side, level = lax.axis_index("xl"), lax.axis_index("z")
    level_word = level.astype(jnp.int32).reshape(1)
    core_word = core.astype(jnp.int32).reshape(1)

    def levels_at(steps):
        return (level.astype(jnp.int32) + jnp.array(steps, jnp.int32) + depth) % depth

    table = counts.reshape(places, 2, 2, depth, experts)
    line_counts = lax.dynamic_slice(
        table, (place, core, side, 0, 0), (1, 1, 1, depth, experts)
    ).reshape(depth, experts)
    near_counts = lax.dynamic_slice_in_dim(jnp.concatenate([line_counts] * 2), level, depth, 0)
    near_counts = jnp.stack([near_counts[by % depth] for by in order])
    near_hot = slot_hot(near_counts, slots, rows)
    hot_at = {by: near_hot[i] for i, by in enumerate(order)}
    own_hot = near_hot[0].reshape(experts * slots, rows)

    other_codes, other_scales = lax.ppermute((codes[0], scales[0]), "xl", SWAP)
    by_level = split_levels(hidden, level_word, depth)

    packed = jnp.stack(
        [
            jnp.dot(own_hot, cotangent[:, c * half : (c + 1) * half],
                    preferred_element_type=jnp.float32).astype(jnp.bfloat16)
            for c in range(2)
        ]
    ).reshape(2 * experts, slots, half)
    arrived = lax.all_to_all(packed, ("c",) + PLACES, 0, 0)
    values = lax.all_gather(arrived.reshape(2 * places * slots, half), "z", axis=0, tiled=True)
    values = values.reshape(depth, 2, places * slots, half)

    line_hidden = {}
    for block, by in zip(by_level, order):
        line_hidden[-by if by < depth // 2 else by] = along_z(block, by) if by else block
    line_hidden = after([line_hidden[by] for by in order], arrived)
    hidden_slots = jnp.einsum("zesr,zrw->ezsw", near_hot, jnp.stack(line_hidden),
                              preferred_element_type=jnp.float32).astype(jnp.bfloat16)
    own_hidden = lax.all_to_all(hidden_slots, PLACES, 0, 0)
    mate_hidden = lax.ppermute(own_hidden, "c", SWAP)
    all_hidden = order_hidden(levels_at(order), core_word, own_hidden, mate_hidden)

    other_codes, other_scales = after((other_codes, other_scales), arrived)
    first = side == 0
    both_codes = jnp.where(first, jnp.stack([codes[0], other_codes]),
                           jnp.stack([other_codes, codes[0]])).reshape(wide, half).T
    both_scales = jnp.where(first, jnp.stack([scales[0], other_scales]),
                            jnp.stack([other_scales, scales[0]])).reshape(1, wide)

    chunks = far_first(depth)
    mates = [
        lax.ppermute(
            partials(levels_at(steps), core_word, values, both_codes, both_scales), "c", SWAP
        )
        for steps in chunks
    ]
    came = {}
    for steps, mate in zip(chunks, mates):
        joined = partials(
            levels_at(steps), core_word, values, both_codes, both_scales, mate, places
        )
        back = lax.all_to_all(joined, PLACES, 0, 0)
        hot = jnp.stack([hot_at[by] for by in steps])
        line_back = jnp.einsum("zesr,ezsw->zrw", hot, back,
                               preferred_element_type=jnp.float32).astype(jnp.bfloat16)
        for i, by in enumerate(steps):
            came[-by if by < depth // 2 else by] = along_z(line_back[i], by) if by else line_back[i]
    d_hidden = join_levels([came[by] for by in order], level_word)

    all_hidden = after(all_hidden, joined)
    sums = lax.dot_general(
        all_hidden.reshape(-1, wide), values.reshape(-1, half), (((0,), (0,)), ((), ())),
        preferred_element_type=jnp.float32,
    ).reshape(2, share, half)
    gone = lax.dynamic_index_in_dim(sums, 1 - side, 0, keepdims=False)
    kept = lax.dynamic_index_in_dim(sums, side, 0, keepdims=False)
    weight_grad = kept + lax.ppermute(gone, "xl", SWAP)
    return d_hidden, weight_grad[None]


def solution(mesh):
    lanes, lines = mesh.devices.shape
    fine = Mesh(mesh.devices.reshape(2, lanes // 4, 2, 2, lines // 2), ("xh", "y", "c", "xl", "z"))
    expert, dp = ("xh", "y", "c"), ("xl", "z")
    in_specs = (P(expert + dp, None), P(expert + dp, None), P(expert, dp, None), P(expert, dp), P())
    out_specs = (P(expert + dp, None), P(expert, dp, None))
    return jax.shard_map(shards, mesh=fine, in_specs=in_specs, out_specs=out_specs, check_vma=False)
```

```python
import jax
import jax.numpy as jnp
from jax import lax
from jax.experimental import pallas as pl
from jax.experimental.pallas import tpu as pltpu
from jax.sharding import Mesh, PartitionSpec as P

PLACES = ("xh", "y")
SWAP = [(0, 1), (1, 0)]


def slot_hot(row_counts, slots, rows):
    starts = jnp.cumsum(row_counts, axis=-1) - row_counts
    slot = jnp.arange(slots, dtype=jnp.int32)
    source = jnp.where(slot < row_counts[..., None], starts[..., None] + slot, -1)
    return (source[..., None] == jnp.arange(rows, dtype=jnp.int32)).astype(jnp.bfloat16)


def distances(depth):
    near = [0]
    for k in range(1, depth // 2):
        near += [-k, k]
    return near + [depth // 2]


def far_first(depth):
    order = distances(depth)[::-1]
    return [order[:3], order[3:]]


def after(value, *others):
    return lax.optimization_barrier((value,) + others)[0]


def along_z(value, by):
    depth = lax.axis_size("z")
    return lax.ppermute(value, "z", [(i, (i + by) % depth) for i in range(depth)])


def split_kernel(level_ref, hidden_ref, *refs):
    outs, held = refs[:-1], refs[-1]
    depth, _, wide = held.shape
    share = wide // 2
    for z in range(depth):
        low = hidden_ref[:, z * share : (z + 1) * share]
        high = hidden_ref[:, (depth + z) * share : (depth + z + 1) * share]
        held[z] = jnp.concatenate([low, high], axis=1)
    for out, by in zip(outs, distances(depth)):
        out[...] = held[lax.rem(level_ref[0] + (by + depth), depth)]


def split_levels(hidden, level, depth):
    rows, width = hidden.shape
    block = (rows, width // depth)
    whole = pl.BlockSpec(memory_space=pltpu.VMEM)
    return pl.pallas_call(
        split_kernel,
        out_shape=[jax.ShapeDtypeStruct(block, hidden.dtype)] * depth,
        in_specs=[pl.BlockSpec(memory_space=pltpu.SMEM), whole],
        out_specs=[whole] * depth,
        scratch_shapes=[pltpu.VMEM((depth,) + block, hidden.dtype)],
        compiler_params=pltpu.CompilerParams(vmem_limit_bytes=56 << 20),
        cost_estimate=pl.CostEstimate(flops=0, bytes_accessed=4 * rows * width, transcendentals=0),
    )(level, hidden)


def join_kernel(level_ref, *refs):
    parts, out_ref, held = refs[:-2], refs[-2], refs[-1]
    depth, _, wide = held.shape
    share = wide // 2
    for part, by in zip(parts, distances(depth)):
        held[lax.rem(level_ref[0] + (by + depth), depth)] = part[...]
    for z in range(0, depth, 2):
        for s in range(2):
            pair = [held[z + i, :, s * share : (s + 1) * share] for i in range(2)]
            out_ref[:, (s * depth + z) * share : (s * depth + z + 2) * share] = (
                jnp.concatenate(pair, axis=1)
            )


def join_levels(parts, level):
    depth = len(parts)
    rows, wide = parts[0].shape
    whole = pl.BlockSpec(memory_space=pltpu.VMEM)
    return pl.pallas_call(
        join_kernel,
        out_shape=jax.ShapeDtypeStruct((rows, depth * wide), parts[0].dtype),
        in_specs=[pl.BlockSpec(memory_space=pltpu.SMEM)] + [whole] * depth,
        out_specs=whole,
        scratch_shapes=[pltpu.VMEM((depth, rows, wide), parts[0].dtype)],
        compiler_params=pltpu.CompilerParams(vmem_limit_bytes=56 << 20),
        cost_estimate=pl.CostEstimate(
            flops=0, bytes_accessed=4 * rows * depth * wide, transcendentals=0
        ),
    )(level, *parts)


def mate_kernel(place_ref, core_ref, rows_ref, codes_ref, scales_ref, out_ref):
    out_ref[0] = scales_ref[...] * jnp.dot(
        rows_ref[0, 0], codes_ref[...], preferred_element_type=jnp.float32
    )


def own_kernel(place_ref, core_ref, rows_ref, codes_ref, scales_ref, mate_ref, out_ref):
    total = mate_ref[0] + scales_ref[...] * jnp.dot(
        rows_ref[0, 0], codes_ref[...], preferred_element_type=jnp.float32
    )
    places, _, slots, wide = out_ref.shape
    out_ref[:, 0] = total.reshape(places, slots, wide).astype(out_ref.dtype)


def partials(where, core, values, codes, scales, mate=None, places=None):
    steps = where.shape[0]
    _, _, rows, half = values.shape
    wide = codes.shape[1]
    flip = 1 if mate is None else 0
    f32 = jax.ShapeDtypeStruct((steps, rows, wide), jnp.float32)
    in_specs = [
        pl.BlockSpec((1, 1, rows, half), lambda j, w, c: (w[j], c[0] ^ flip, 0, 0)),
        pl.BlockSpec((half, wide), lambda j, w, c: (0, 0)),
        pl.BlockSpec((1, wide), lambda j, w, c: (0, 0)),
    ]
    row_spec = pl.BlockSpec((1, rows, wide), lambda j, w, c: (j, 0, 0))
    if mate is None:
        kernel, out_shape, out_spec, extra = mate_kernel, f32, row_spec, ()
    else:
        slots = rows // places
        kernel, extra = own_kernel, (mate,)
        in_specs.append(row_spec)
        out_shape = jax.ShapeDtypeStruct((places, steps, slots, wide), jnp.bfloat16)
        out_spec = pl.BlockSpec((places, 1, slots, wide), lambda j, w, c: (0, j, 0, 0))
    return pl.pallas_call(
        kernel,
        out_shape=out_shape,
        grid_spec=pltpu.PrefetchScalarGridSpec(
            num_scalar_prefetch=2, grid=(steps,), in_specs=in_specs, out_specs=out_spec
        ),
        compiler_params=pltpu.CompilerParams(vmem_limit_bytes=56 << 20),
        cost_estimate=pl.CostEstimate(
            flops=2 * steps * rows * half * wide,
            bytes_accessed=steps * rows * (2 * half + 8 * wide),
            transcendentals=0,
        ),
    )(where, core, values, codes, scales, *extra)


def order_kernel(where_ref, core_ref, own_ref, mate_ref, out_ref):
    me = core_ref[0]
    out_ref[0, me] = own_ref[:, 0]
    out_ref[0, 1 - me] = mate_ref[:, 0]


def order_hidden(where, core, own, mate):
    places, depth, slots, wide = own.shape
    in_spec = pl.BlockSpec((places, 1, slots, wide), lambda j, w, c: (0, j, 0, 0))
    return pl.pallas_call(
        order_kernel,
        out_shape=jax.ShapeDtypeStruct((depth, 2, places, slots, wide), own.dtype),
        grid_spec=pltpu.PrefetchScalarGridSpec(
            num_scalar_prefetch=2,
            grid=(depth,),
            in_specs=[in_spec, in_spec],
            out_specs=pl.BlockSpec((1, 2, places, slots, wide), lambda j, w, c: (w[j], 0, 0, 0, 0)),
        ),
        compiler_params=pltpu.CompilerParams(vmem_limit_bytes=56 << 20),
        cost_estimate=pl.CostEstimate(
            flops=0, bytes_accessed=8 * places * depth * slots * wide, transcendentals=0
        ),
    )(where, core, own, mate)


def shards(cotangent, hidden, codes, scales, counts):
    rows, cols = cotangent.shape
    half = cols // 2
    share = codes.shape[1]
    places = lax.axis_size(PLACES)
    depth = lax.axis_size("z")
    experts = counts.shape[1]
    slots = 3 * rows // (2 * experts)
    wide = 2 * share
    order = distances(depth)
    place, core = lax.axis_index(PLACES), lax.axis_index("c")
    side, level = lax.axis_index("xl"), lax.axis_index("z")
    level_word = level.astype(jnp.int32).reshape(1)
    core_word = core.astype(jnp.int32).reshape(1)

    def levels_at(steps):
        return (level.astype(jnp.int32) + jnp.array(steps, jnp.int32) + depth) % depth

    table = counts.reshape(places, 2, 2, depth, experts)
    line_counts = lax.dynamic_slice(
        table, (place, core, side, 0, 0), (1, 1, 1, depth, experts)
    ).reshape(depth, experts)
    near_counts = lax.dynamic_slice_in_dim(jnp.concatenate([line_counts] * 2), level, depth, 0)
    near_counts = jnp.stack([near_counts[by % depth] for by in order])
    near_hot = slot_hot(near_counts, slots, rows)
    hot_at = {by: near_hot[i] for i, by in enumerate(order)}
    own_hot = near_hot[0].reshape(experts * slots, rows)

    other_codes, other_scales = lax.ppermute((codes[0], scales[0]), "xl", SWAP)
    by_level = split_levels(hidden, level_word, depth)

    packed = jnp.stack(
        [
            jnp.dot(own_hot, cotangent[:, c * half : (c + 1) * half],
                    preferred_element_type=jnp.float32).astype(jnp.bfloat16)
            for c in range(2)
        ]
    ).reshape(2 * experts, slots, half)
    arrived = lax.all_to_all(packed, ("c",) + PLACES, 0, 0)

    line_hidden = {}
    for block, by in zip(by_level, order):
        line_hidden[-by if by < depth // 2 else by] = along_z(block, by) if by else block
    near = [line_hidden[by] for by in order[1:5]]
    arrived, other_codes, other_scales, *near = lax.optimization_barrier(
        [arrived, other_codes, other_scales] + near
    )
    line_hidden.update(zip(order[1:5], near))
    values = lax.all_gather(arrived.reshape(2 * places * slots, half), "z", axis=0, tiled=True)
    values = values.reshape(depth, 2, places * slots, half)

    line_hidden = [line_hidden[by] for by in order]
    hidden_slots = jnp.einsum("zesr,zrw->ezsw", near_hot, jnp.stack(line_hidden),
                              preferred_element_type=jnp.float32).astype(jnp.bfloat16)
    own_hidden = lax.all_to_all(hidden_slots, PLACES, 0, 0)
    mate_hidden = lax.ppermute(own_hidden, "c", SWAP)
    all_hidden = order_hidden(levels_at(order), core_word, own_hidden, mate_hidden)
    hidden_t = all_hidden.reshape(-1, wide).T.reshape(2, share, -1)
    gone_t = lax.dynamic_index_in_dim(hidden_t, 1 - side, 0, keepdims=False)
    kept_t = lax.dynamic_index_in_dim(hidden_t, side, 0, keepdims=False)
    values, gone_t, kept_t = lax.optimization_barrier((values, gone_t, kept_t))
    flat_values = values.reshape(-1, half)

    first = side == 0
    both_codes = jnp.where(first, jnp.stack([codes[0], other_codes]),
                           jnp.stack([other_codes, codes[0]])).reshape(wide, half).T
    both_scales = jnp.where(first, jnp.stack([scales[0], other_scales]),
                            jnp.stack([other_scales, scales[0]])).reshape(1, wide)

    def weight(units_t):
        return jnp.dot(units_t, flat_values, preferred_element_type=jnp.float32)

    def mate_partials(where):
        return partials(where, core_word, values, both_codes, both_scales)

    def join(where, mate):
        return partials(where, core_word, values, both_codes, both_scales, mate, places)

    def unpack(steps, back):
        hot = jnp.stack([hot_at[by] for by in steps])
        return jnp.einsum("zesr,ezsw->zrw", hot, back,
                          preferred_element_type=jnp.float32).astype(jnp.bfloat16)

    far, close = far_first(depth)
    far_at, close_at = levels_at(far), levels_at(close)
    far_mate = mate_partials(far_at)
    gone = weight(after(gone_t, far_mate))
    weight_in = lax.ppermute(gone, "xl", SWAP)
    far_joined = join(after(far_at, gone), lax.ppermute(far_mate, "c", SWAP))
    close_mate = mate_partials(after(close_at, far_joined))
    close_joined = join(close_at, lax.ppermute(close_mate, "c", SWAP))
    far_back = unpack(far, after(lax.all_to_all(far_joined, PLACES, 0, 0), close_joined))
    close_back = unpack(close, lax.all_to_all(close_joined, PLACES, 0, 0))
    came = {}
    for steps, back in ((far, far_back), (close, close_back)):
        for i, by in enumerate(steps):
            came[-by if by < depth // 2 else by] = along_z(back[i], by) if by else back[i]
    weight_grad = weight_in + weight(after(kept_t, weight_in, close_back))
    d_hidden = join_levels([came[by] for by in order], after(level_word, weight_grad))
    return d_hidden, weight_grad[None]


def solution(mesh):
    lanes, lines = mesh.devices.shape
    fine = Mesh(mesh.devices.reshape(2, lanes // 4, 2, 2, lines // 2), ("xh", "y", "c", "xl", "z"))
    expert, dp = ("xh", "y", "c"), ("xl", "z")
    in_specs = (P(expert + dp, None), P(expert + dp, None), P(expert, dp, None), P(expert, dp), P())
    out_specs = (P(expert + dp, None), P(expert, dp, None))
    return jax.shard_map(shards, mesh=fine, in_specs=in_specs, out_specs=out_specs, check_vma=False)
```

```python
import jax
import jax.numpy as jnp
from jax import lax
from jax.experimental import pallas as pl
from jax.experimental.pallas import tpu as pltpu
from jax.sharding import Mesh, PartitionSpec as P

PLACES = ("xh", "y")
SWAP = [(0, 1), (1, 0)]


def slot_hot(row_counts, slots, rows):
    starts = jnp.cumsum(row_counts, axis=-1) - row_counts
    slot = jnp.arange(slots, dtype=jnp.int32)
    source = jnp.where(slot < row_counts[..., None], starts[..., None] + slot, -1)
    return (source[..., None] == jnp.arange(rows, dtype=jnp.int32)).astype(jnp.bfloat16)


def distances(depth):
    order = [depth // 2]
    for k in range(depth // 2 - 1, 0, -1):
        order += [k, -k]
    return order + [0]


def after(value, *others):
    return lax.optimization_barrier((value,) + others)[0]


def along_z(value, by):
    depth = lax.axis_size("z")
    return lax.ppermute(value, "z", [(i, (i + by) % depth) for i in range(depth)])


def split_kernel(level_ref, hidden_ref, *refs):
    outs, held = refs[:-1], refs[-1]
    depth, _, wide = held.shape
    share = wide // 2
    for z in range(depth):
        low = hidden_ref[:, z * share : (z + 1) * share]
        high = hidden_ref[:, (depth + z) * share : (depth + z + 1) * share]
        held[z] = jnp.concatenate([low, high], axis=1)
    for out, by in zip(outs, distances(depth)):
        out[...] = held[lax.rem(level_ref[0] + (by + depth), depth)]


def split_levels(hidden, level, depth):
    rows, width = hidden.shape
    block = (rows, width // depth)
    whole = pl.BlockSpec(memory_space=pltpu.VMEM)
    return pl.pallas_call(
        split_kernel,
        out_shape=[jax.ShapeDtypeStruct(block, hidden.dtype)] * depth,
        in_specs=[pl.BlockSpec(memory_space=pltpu.SMEM), whole],
        out_specs=[whole] * depth,
        scratch_shapes=[pltpu.VMEM((depth,) + block, hidden.dtype)],
        compiler_params=pltpu.CompilerParams(vmem_limit_bytes=40 << 20),
        cost_estimate=pl.CostEstimate(flops=0, bytes_accessed=4 * rows * width, transcendentals=0),
    )(level, hidden)


def join_kernel(level_ref, *refs):
    parts, out_ref, held = refs[:-2], refs[-2], refs[-1]
    depth, _, wide = held.shape
    share = wide // 2
    for part, by in zip(parts, distances(depth)):
        held[lax.rem(level_ref[0] + (by + depth), depth)] = part[...]
    for z in range(0, depth, 2):
        for s in range(2):
            pair = [held[z + i, :, s * share : (s + 1) * share] for i in range(2)]
            out_ref[:, (s * depth + z) * share : (s * depth + z + 2) * share] = (
                jnp.concatenate(pair, axis=1)
            )


def join_levels(parts, level):
    depth = len(parts)
    rows, wide = parts[0].shape
    whole = pl.BlockSpec(memory_space=pltpu.VMEM)
    return pl.pallas_call(
        join_kernel,
        out_shape=jax.ShapeDtypeStruct((rows, depth * wide), parts[0].dtype),
        in_specs=[pl.BlockSpec(memory_space=pltpu.SMEM)] + [whole] * depth,
        out_specs=whole,
        scratch_shapes=[pltpu.VMEM((depth, rows, wide), parts[0].dtype)],
        compiler_params=pltpu.CompilerParams(vmem_limit_bytes=40 << 20),
        cost_estimate=pl.CostEstimate(
            flops=0, bytes_accessed=4 * rows * depth * wide, transcendentals=0
        ),
    )(level, *parts)


def mate_kernel(place_ref, codes_ref, scales_ref, *refs):
    rows_refs, out_ref = refs[:-1], refs[-1]
    values = jnp.concatenate([ref[0, 0] for ref in rows_refs])
    out_ref[...] = scales_ref[...] * jnp.dot(
        values, codes_ref[...], preferred_element_type=jnp.float32
    )


def own_kernel(place_ref, codes_ref, scales_ref, *refs):
    rows_refs, mate_ref, out_ref = refs[:-2], refs[-2], refs[-1]
    values = jnp.concatenate([ref[0, 0] for ref in rows_refs])
    total = mate_ref[...] + scales_ref[...] * jnp.dot(
        values, codes_ref[...], preferred_element_type=jnp.float32
    )
    places, steps, slots, wide = out_ref.shape
    total = total.reshape(steps, places, slots, wide).astype(out_ref.dtype)
    for step in range(steps):
        out_ref[:, step] = total[step]


def partials(where, values, codes, scales, mate=None, places=None):
    steps = where.shape[0]
    _, _, rows, half = values.shape
    wide = codes.shape[1]
    flip = 1 if mate is None else 0

    def rows_spec(j):
        return pl.BlockSpec((1, 1, rows, half), lambda i, w: (w[j], flip, 0, 0))

    def whole(*shape):
        return pl.BlockSpec(shape, lambda i, w: (0,) * len(shape))

    in_specs = [whole(half, wide), whole(1, wide)] + [rows_spec(j) for j in range(steps)]
    if mate is None:
        kernel, shape, dtype, extra = mate_kernel, (steps * rows, wide), jnp.float32, ()
    else:
        kernel, extra = own_kernel, (mate,)
        in_specs.append(whole(steps * rows, wide))
        shape, dtype = (places, steps, rows // places, wide), jnp.bfloat16
    return pl.pallas_call(
        kernel,
        out_shape=jax.ShapeDtypeStruct(shape, dtype),
        grid_spec=pltpu.PrefetchScalarGridSpec(
            num_scalar_prefetch=1, grid=(1,), in_specs=in_specs, out_specs=whole(*shape)
        ),
        compiler_params=pltpu.CompilerParams(vmem_limit_bytes=40 << 20),
        cost_estimate=pl.CostEstimate(
            flops=2 * steps * rows * half * wide,
            bytes_accessed=steps * rows * (2 * half + 8 * wide),
            transcendentals=0,
        ),
    )(where, codes, scales, *[values] * steps, *extra)


def pack_kernel(level_ref, hot_ref, *refs):
    blocks, out_ref = refs[:-1], refs[-1]
    experts, depth, slots, wide = out_ref.shape
    for i, by in enumerate(distances(depth)):
        packed = jnp.dot(hot_ref[i], blocks[i][...], preferred_element_type=jnp.float32)
        level = lax.rem(level_ref[0] + (by + depth), depth)
        out_ref[:, level] = packed.reshape(experts, slots, wide).astype(out_ref.dtype)


def pack_hidden(hot, blocks, level, experts):
    depth, places, rows = hot.shape
    wide = blocks[0].shape[1]
    whole = pl.BlockSpec(memory_space=pltpu.VMEM)
    return pl.pallas_call(
        pack_kernel,
        out_shape=jax.ShapeDtypeStruct((experts, depth, places // experts, wide), jnp.bfloat16),
        in_specs=[pl.BlockSpec(memory_space=pltpu.SMEM)] + [whole] * (depth + 1),
        out_specs=whole,
        compiler_params=pltpu.CompilerParams(vmem_limit_bytes=32 << 20),
        cost_estimate=pl.CostEstimate(
            flops=2 * depth * places * rows * wide,
            bytes_accessed=2 * depth * (places + rows) * wide,
            transcendentals=0,
        ),
    )(level, hot, *blocks)


def shards(cotangent, hidden, codes, scales, counts):
    rows, cols = cotangent.shape
    half = cols // 2
    share = codes.shape[1]
    places = lax.axis_size(PLACES)
    depth = lax.axis_size("z")
    experts = counts.shape[1]
    slots = 3 * rows // (2 * experts)
    wide = 2 * share
    order = distances(depth)
    place, core = lax.axis_index(PLACES), lax.axis_index("c")
    side, level = lax.axis_index("xl"), lax.axis_index("z")
    level_word = level.astype(jnp.int32).reshape(1)

    def levels_at(steps):
        return (level.astype(jnp.int32) + jnp.array(steps, jnp.int32) + depth) % depth

    table = counts.reshape(places, 2, 2, depth, experts)
    line_counts = lax.dynamic_slice(
        table, (place, core, side, 0, 0), (1, 1, 1, depth, experts)
    ).reshape(depth, experts)
    near_counts = lax.dynamic_slice_in_dim(jnp.concatenate([line_counts] * 2), level, depth, 0)
    near_counts = jnp.stack([near_counts[by % depth] for by in order])
    near_hot = slot_hot(near_counts, slots, rows)
    own_hot = near_hot[-1].reshape(experts * slots, rows)

    other_codes, other_scales = lax.ppermute((codes[0], scales[0]), "xl", SWAP)
    by_level = split_levels(hidden, level_word, depth)

    packed = jnp.stack(
        [
            jnp.dot(own_hot, cotangent[:, c * half : (c + 1) * half],
                    preferred_element_type=jnp.float32).astype(jnp.bfloat16)
            for c in range(2)
        ]
    ).reshape(2 * experts, slots, half)
    arrived = lax.all_to_all(packed, ("c",) + PLACES, 0, 0).reshape(2, places * slots, half)

    line_hidden = {}
    for block, by in zip(by_level, order):
        line_hidden[-by if by < depth // 2 else by] = along_z(block, by) if by else block
    arrived, line_hidden[-1], line_hidden[1] = lax.optimization_barrier(
        (arrived, line_hidden[-1], line_hidden[1])
    )
    arrived = jnp.where(core == 0, arrived, arrived[::-1])
    values = lax.all_gather(arrived.reshape(2 * places * slots, half), "z", axis=0, tiled=True)
    values = values.reshape(depth, 2, places * slots, half)

    first = side == 0
    both_codes = jnp.where(first, jnp.stack([codes[0], other_codes]),
                           jnp.stack([other_codes, codes[0]])).reshape(wide, half).T
    both_scales = jnp.where(first, jnp.stack([scales[0], other_scales]),
                            jnp.stack([other_scales, scales[0]])).reshape(1, wide)
    both_codes, both_scales, *line_hidden = lax.optimization_barrier(
        [both_codes, both_scales] + [line_hidden[by] for by in order]
    )

    hidden_slots = pack_hidden(
        near_hot.reshape(depth, experts * slots, rows), line_hidden, level_word, experts
    )
    own_hidden = lax.all_to_all(hidden_slots, PLACES, 0, 0)
    own_hidden = own_hidden.transpose(1, 0, 2, 3).reshape(depth * places * slots, wide)
    mate_hidden = lax.ppermute(own_hidden, "c", SWAP)
    values = after(values, own_hidden)

    def weight(units, rows_of):
        return lax.dot_general(
            units, values[:, rows_of].reshape(-1, half), (((0,), (0,)), ((), ())),
            preferred_element_type=jnp.float32,
        )

    def mate_partials(where):
        return partials(where, values, both_codes, both_scales)

    def join(where, mate):
        return partials(where, values, both_codes, both_scales, mate, places)

    def unpack(hot, back):
        return jnp.einsum("zesr,ezsw->zrw", hot, back,
                          preferred_element_type=jnp.float32).astype(jnp.bfloat16)

    came = {}

    def send_home(steps, back):
        blocks = lax.optimization_barrier([back[i] for i in range(len(steps))])
        for by, block in zip(steps, blocks):
            came[-by if by < depth // 2 else by] = along_z(block, by) if by else block
        return blocks

    cut = 3
    far_at, close_at = levels_at(order[:cut]), levels_at(order[cut:])
    far_joined = join(far_at, lax.ppermute(mate_partials(far_at), "c", SWAP))
    close_mate = mate_partials(after(close_at, far_joined))
    close_joined = join(close_at, lax.ppermute(close_mate, "c", SWAP))
    far_raw = after(lax.all_to_all(far_joined, PLACES, 0, 0), close_joined)
    far_back = send_home(order[:cut], unpack(near_hot[:cut], far_raw))
    close_raw = lax.all_to_all(close_joined, PLACES, 0, 0)
    close_raw = after(close_raw, *came.values())
    send_home(order[cut:], unpack(near_hot[cut:], close_raw))

    own_hidden, mate_hidden = after((own_hidden, mate_hidden), *far_back)
    sums = (weight(own_hidden, 0) + weight(mate_hidden, 1)).reshape(2, share, half)
    gone = lax.dynamic_index_in_dim(sums, 1 - side, 0, keepdims=False)
    kept = lax.dynamic_index_in_dim(sums, side, 0, keepdims=False)
    largest = jnp.maximum(jnp.max(jnp.abs(gone)), 1e-30).reshape(1)
    gone = (gone * (1 / largest)).astype(jnp.float16)
    gone, largest, kept, _ = lax.optimization_barrier((gone, largest, kept, close_raw))
    gone, largest = lax.ppermute((gone, largest), "xl", SWAP)
    weight_grad = kept + gone.astype(jnp.float32) * largest
    d_hidden = join_levels([came[by] for by in order], after(level_word, weight_grad))
    return d_hidden, weight_grad[None]


def solution(mesh):
    lanes, lines = mesh.devices.shape
    fine = Mesh(mesh.devices.reshape(2, lanes // 4, 2, 2, lines // 2), ("xh", "y", "c", "xl", "z"))
    expert, dp = ("xh", "y", "c"), ("xl", "z")
    in_specs = (P(expert + dp, None), P(expert + dp, None), P(expert, dp, None), P(expert, dp), P())
    out_specs = (P(expert + dp, None), P(expert, dp, None))
    return jax.shard_map(shards, mesh=fine, in_specs=in_specs, out_specs=out_specs, check_vma=False)
```

```python
import jax
import jax.numpy as jnp
from jax import lax
from jax.experimental import pallas as pl
from jax.experimental.pallas import tpu as pltpu
from jax.sharding import Mesh, PartitionSpec as P

PLACES = ("xh", "y")
SWAP = [(0, 1), (1, 0)]


def slot_hot(row_counts, slots, rows):
    starts = jnp.cumsum(row_counts, axis=-1) - row_counts
    slot = jnp.arange(slots, dtype=jnp.int32)
    source = jnp.where(slot < row_counts[..., None], starts[..., None] + slot, -1)
    return (source[..., None] == jnp.arange(rows, dtype=jnp.int32)).astype(jnp.bfloat16)


def distances(depth):
    order = [depth // 2]
    for k in range(depth // 2 - 1, 0, -1):
        order += [k, -k]
    return order + [0]


def after(value, *others):
    return lax.optimization_barrier((value,) + others)[0]


def along_z(value, by):
    depth = lax.axis_size("z")
    return lax.ppermute(value, "z", [(i, (i + by) % depth) for i in range(depth)])


def split_kernel(level_ref, hidden_ref, *refs):
    outs, held = refs[:-1], refs[-1]
    depth, _, wide = held.shape
    share = wide // 2
    for z in range(depth):
        low = hidden_ref[:, z * share : (z + 1) * share]
        high = hidden_ref[:, (depth + z) * share : (depth + z + 1) * share]
        held[z] = jnp.concatenate([low, high], axis=1)
    for out, by in zip(outs, distances(depth)):
        out[...] = held[lax.rem(level_ref[0] + (by + depth), depth)]


def split_levels(hidden, level, depth):
    rows, width = hidden.shape
    block = (rows, width // depth)
    whole = pl.BlockSpec(memory_space=pltpu.VMEM)
    return pl.pallas_call(
        split_kernel,
        out_shape=[jax.ShapeDtypeStruct(block, hidden.dtype)] * depth,
        in_specs=[pl.BlockSpec(memory_space=pltpu.SMEM), whole],
        out_specs=[whole] * depth,
        scratch_shapes=[pltpu.VMEM((depth,) + block, hidden.dtype)],
        compiler_params=pltpu.CompilerParams(vmem_limit_bytes=40 << 20),
        cost_estimate=pl.CostEstimate(flops=0, bytes_accessed=4 * rows * width, transcendentals=0),
    )(level, hidden)


def join_kernel(level_ref, *refs):
    parts, out_ref, held = refs[:-2], refs[-2], refs[-1]
    depth, _, wide = held.shape
    share = wide // 2
    for part, by in zip(parts, distances(depth)):
        held[lax.rem(level_ref[0] + (by + depth), depth)] = part[...]
    for z in range(0, depth, 2):
        for s in range(2):
            pair = [held[z + i, :, s * share : (s + 1) * share] for i in range(2)]
            out_ref[:, (s * depth + z) * share : (s * depth + z + 2) * share] = (
                jnp.concatenate(pair, axis=1)
            )


def join_levels(parts, level):
    depth = len(parts)
    rows, wide = parts[0].shape
    whole = pl.BlockSpec(memory_space=pltpu.VMEM)
    return pl.pallas_call(
        join_kernel,
        out_shape=jax.ShapeDtypeStruct((rows, depth * wide), parts[0].dtype),
        in_specs=[pl.BlockSpec(memory_space=pltpu.SMEM)] + [whole] * depth,
        out_specs=whole,
        scratch_shapes=[pltpu.VMEM((depth, rows, wide), parts[0].dtype)],
        compiler_params=pltpu.CompilerParams(vmem_limit_bytes=40 << 20),
        cost_estimate=pl.CostEstimate(
            flops=0, bytes_accessed=4 * rows * depth * wide, transcendentals=0
        ),
    )(level, *parts)


def mate_kernel(place_ref, core_ref, codes_ref, scales_ref, *refs):
    rows_refs, out_ref = refs[:-1], refs[-1]
    values = jnp.concatenate([ref[0, 0] for ref in rows_refs])
    out_ref[...] = scales_ref[...] * jnp.dot(
        values, codes_ref[...], preferred_element_type=jnp.float32
    )


def own_kernel(place_ref, core_ref, codes_ref, scales_ref, *refs):
    rows_refs, mate_ref, out_ref = refs[:-2], refs[-2], refs[-1]
    values = jnp.concatenate([ref[0, 0] for ref in rows_refs])
    total = mate_ref[...] + scales_ref[...] * jnp.dot(
        values, codes_ref[...], preferred_element_type=jnp.float32
    )
    places, steps, slots, wide = out_ref.shape
    total = total.reshape(steps, places, slots, wide).astype(out_ref.dtype)
    for step in range(steps):
        out_ref[:, step] = total[step]


def partials(where, core, values, codes, scales, mate=None, places=None):
    steps = where.shape[0]
    _, _, rows, half = values.shape
    wide = codes.shape[1]
    flip = 1 if mate is None else 0

    def rows_spec(j):
        return pl.BlockSpec((1, 1, rows, half), lambda i, w, c: (w[j], c[0] ^ flip, 0, 0))

    def whole(*shape):
        return pl.BlockSpec(shape, lambda i, w, c: (0,) * len(shape))

    in_specs = [whole(half, wide), whole(1, wide)] + [rows_spec(j) for j in range(steps)]
    if mate is None:
        kernel, shape, dtype, extra = mate_kernel, (steps * rows, wide), jnp.float32, ()
    else:
        kernel, extra = own_kernel, (mate,)
        in_specs.append(whole(steps * rows, wide))
        shape, dtype = (places, steps, rows // places, wide), jnp.bfloat16
    return pl.pallas_call(
        kernel,
        out_shape=jax.ShapeDtypeStruct(shape, dtype),
        grid_spec=pltpu.PrefetchScalarGridSpec(
            num_scalar_prefetch=2, grid=(1,), in_specs=in_specs, out_specs=whole(*shape)
        ),
        compiler_params=pltpu.CompilerParams(vmem_limit_bytes=40 << 20),
        cost_estimate=pl.CostEstimate(
            flops=2 * steps * rows * half * wide,
            bytes_accessed=steps * rows * (2 * half + 8 * wide),
            transcendentals=0,
        ),
    )(where, core, codes, scales, *[values] * steps, *extra)


def pack_kernel(level_ref, hot_ref, *refs):
    blocks, out_ref = refs[:-1], refs[-1]
    experts, depth, slots, wide = out_ref.shape
    for i, by in enumerate(distances(depth)):
        packed = jnp.dot(hot_ref[i], blocks[i][...], preferred_element_type=jnp.float32)
        level = lax.rem(level_ref[0] + (by + depth), depth)
        out_ref[:, level] = packed.reshape(experts, slots, wide).astype(out_ref.dtype)


def pack_hidden(hot, blocks, level, experts):
    depth, places, rows = hot.shape
    wide = blocks[0].shape[1]
    whole = pl.BlockSpec(memory_space=pltpu.VMEM)
    return pl.pallas_call(
        pack_kernel,
        out_shape=jax.ShapeDtypeStruct((experts, depth, places // experts, wide), jnp.bfloat16),
        in_specs=[pl.BlockSpec(memory_space=pltpu.SMEM)] + [whole] * (depth + 1),
        out_specs=whole,
        compiler_params=pltpu.CompilerParams(vmem_limit_bytes=32 << 20),
        cost_estimate=pl.CostEstimate(
            flops=2 * depth * places * rows * wide,
            bytes_accessed=2 * depth * (places + rows) * wide,
            transcendentals=0,
        ),
    )(level, hot, *blocks)


def shards(cotangent, hidden, codes, scales, counts):
    rows, cols = cotangent.shape
    half = cols // 2
    share = codes.shape[1]
    places = lax.axis_size(PLACES)
    depth = lax.axis_size("z")
    experts = counts.shape[1]
    slots = 3 * rows // (2 * experts)
    wide = 2 * share
    order = distances(depth)
    place, core = lax.axis_index(PLACES), lax.axis_index("c")
    side, level = lax.axis_index("xl"), lax.axis_index("z")
    core_word = core.astype(jnp.int32).reshape(1)
    level_word = level.astype(jnp.int32).reshape(1)

    def levels_at(steps):
        return (level.astype(jnp.int32) + jnp.array(steps, jnp.int32) + depth) % depth

    table = counts.reshape(places, 2, 2, depth, experts)
    line_counts = lax.dynamic_slice(
        table, (place, core, side, 0, 0), (1, 1, 1, depth, experts)
    ).reshape(depth, experts)
    near_counts = lax.dynamic_slice_in_dim(jnp.concatenate([line_counts] * 2), level, depth, 0)
    near_counts = jnp.stack([near_counts[by % depth] for by in order])
    near_hot = slot_hot(near_counts, slots, rows)
    own_hot = near_hot[-1].reshape(experts * slots, rows)

    other_codes, other_scales = lax.ppermute((codes[0], scales[0]), "xl", SWAP)
    by_level = split_levels(hidden, level_word, depth)

    packed = jnp.stack(
        [
            jnp.dot(own_hot, cotangent[:, c * half : (c + 1) * half],
                    preferred_element_type=jnp.float32).astype(jnp.bfloat16)
            for c in range(2)
        ]
    ).reshape(2 * experts, slots, half)
    arrived = lax.all_to_all(packed, ("c",) + PLACES, 0, 0).reshape(2, places * slots, half)

    line_hidden = {}
    for block, by in zip(by_level, order):
        line_hidden[-by if by < depth // 2 else by] = along_z(block, by) if by else block
    arrived, line_hidden[-1], line_hidden[1] = lax.optimization_barrier(
        (arrived, line_hidden[-1], line_hidden[1])
    )
    values = lax.all_gather(arrived.reshape(2 * places * slots, half), "z", axis=0, tiled=True)
    values = values.reshape(depth, 2, places * slots, half)

    first = side == 0
    both_codes = jnp.where(first, jnp.stack([codes[0], other_codes]),
                           jnp.stack([other_codes, codes[0]])).reshape(wide, half).T
    both_scales = jnp.where(first, jnp.stack([scales[0], other_scales]),
                            jnp.stack([other_scales, scales[0]])).reshape(1, wide)
    both_codes, both_scales, *line_hidden = lax.optimization_barrier(
        [both_codes, both_scales] + [line_hidden[by] for by in order]
    )

    hidden_slots = pack_hidden(
        near_hot.reshape(depth, experts * slots, rows), line_hidden, level_word, experts
    )
    own_hidden = lax.all_to_all(hidden_slots, PLACES, 0, 0)
    own_hidden = own_hidden.transpose(1, 0, 2, 3).reshape(depth * places * slots, wide)
    mate_hidden = lax.ppermute(own_hidden, "c", SWAP)
    values = after(values, own_hidden)

    def weight(units, rows_of):
        part = lax.dynamic_index_in_dim(values, rows_of, 1, keepdims=False)
        return lax.dot_general(
            units, part.reshape(-1, half), (((0,), (0,)), ((), ())),
            preferred_element_type=jnp.float32,
        )

    def mate_partials(where):
        return partials(where, core_word, values, both_codes, both_scales)

    def join(where, mate):
        return partials(where, core_word, values, both_codes, both_scales, mate, places)

    def unpack(hot, back):
        return jnp.einsum("zesr,ezsw->zrw", hot, back,
                          preferred_element_type=jnp.float32).astype(jnp.bfloat16)

    came = {}

    def send_home(steps, back):
        blocks = lax.optimization_barrier([back[i] for i in range(len(steps))])
        for by, block in zip(steps, blocks):
            came[-by if by < depth // 2 else by] = along_z(block, by) if by else block
        return blocks

    cut = 3
    far_at, close_at = levels_at(order[:cut]), levels_at(order[cut:])
    far_joined = join(far_at, lax.ppermute(mate_partials(far_at), "c", SWAP))
    close_mate = mate_partials(after(close_at, far_joined))
    close_joined = join(close_at, lax.ppermute(close_mate, "c", SWAP))
    far_raw = after(lax.all_to_all(far_joined, PLACES, 0, 0), close_joined)
    far_back = send_home(order[:cut], unpack(near_hot[:cut], far_raw))
    close_raw = lax.all_to_all(close_joined, PLACES, 0, 0)
    close_raw = after(close_raw, *came.values())
    send_home(order[cut:], unpack(near_hot[cut:], close_raw))

    own_hidden, mate_hidden = after((own_hidden, mate_hidden), *far_back)
    sums = (weight(own_hidden, core) + weight(mate_hidden, 1 - core)).reshape(2, share, half)
    gone = lax.dynamic_index_in_dim(sums, 1 - side, 0, keepdims=False)
    kept = lax.dynamic_index_in_dim(sums, side, 0, keepdims=False)
    largest = jnp.maximum(jnp.max(jnp.abs(gone)), 1e-30).reshape(1)
    gone = (gone * (1 / largest)).astype(jnp.float16)
    largest = lax.ppermute(largest, "xl", SWAP)
    gone, kept, largest, _ = lax.optimization_barrier((gone, kept, largest, close_raw))
    gone = lax.ppermute(gone, "xl", SWAP)
    weight_grad = kept + gone.astype(jnp.float32) * largest
    d_hidden = join_levels([came[by] for by in order], after(level_word, weight_grad))
    return d_hidden, weight_grad[None]


def solution(mesh):
    lanes, lines = mesh.devices.shape
    fine = Mesh(mesh.devices.reshape(2, lanes // 4, 2, 2, lines // 2), ("xh", "y", "c", "xl", "z"))
    expert, dp = ("xh", "y", "c"), ("xl", "z")
    in_specs = (P(expert + dp, None), P(expert + dp, None), P(expert, dp, None), P(expert, dp), P())
    out_specs = (P(expert + dp, None), P(expert, dp, None))
    return jax.shard_map(shards, mesh=fine, in_specs=in_specs, out_specs=out_specs, check_vma=False)
```

```python
import jax
import jax.numpy as jnp
from jax import lax
from jax.experimental import pallas as pl
from jax.experimental.pallas import tpu as pltpu
from jax.sharding import Mesh, PartitionSpec as P

PLACES = ("xh", "y")
SWAP = [(0, 1), (1, 0)]


def slot_hot(row_counts, slots, rows):
    starts = jnp.cumsum(row_counts, axis=-1) - row_counts
    slot = jnp.arange(slots, dtype=jnp.int32)
    source = jnp.where(slot < row_counts[..., None], starts[..., None] + slot, -1)
    return (source[..., None] == jnp.arange(rows, dtype=jnp.int32)).astype(jnp.bfloat16)


def distances(depth):
    order = [depth // 2]
    for k in range(depth // 2 - 1, 0, -1):
        order += [k, -k]
    return order + [0]


def after(value, *others):
    return lax.optimization_barrier((value,) + others)[0]


def along_z(value, by):
    depth = lax.axis_size("z")
    return lax.ppermute(value, "z", [(i, (i + by) % depth) for i in range(depth)])


def split_kernel(level_ref, hidden_ref, *refs):
    outs, held = refs[:-1], refs[-1]
    depth, _, wide = held.shape
    share = wide // 2
    for z in range(depth):
        low = hidden_ref[:, z * share : (z + 1) * share]
        high = hidden_ref[:, (depth + z) * share : (depth + z + 1) * share]
        held[z] = jnp.concatenate([low, high], axis=1)
    for out, by in zip(outs, distances(depth)):
        out[...] = held[lax.rem(level_ref[0] + (by + depth), depth)]


def split_levels(hidden, level, depth):
    rows, width = hidden.shape
    block = (rows, width // depth)
    whole = pl.BlockSpec(memory_space=pltpu.VMEM)
    return pl.pallas_call(
        split_kernel,
        out_shape=[jax.ShapeDtypeStruct(block, hidden.dtype)] * depth,
        in_specs=[pl.BlockSpec(memory_space=pltpu.SMEM), whole],
        out_specs=[whole] * depth,
        scratch_shapes=[pltpu.VMEM((depth,) + block, hidden.dtype)],
        compiler_params=pltpu.CompilerParams(vmem_limit_bytes=40 << 20),
        cost_estimate=pl.CostEstimate(flops=0, bytes_accessed=4 * rows * width, transcendentals=0),
    )(level, hidden)


def join_kernel(level_ref, *refs):
    parts, out_ref, held = refs[:-2], refs[-2], refs[-1]
    depth, _, wide = held.shape
    share = wide // 2
    for part, by in zip(parts, distances(depth)):
        held[lax.rem(level_ref[0] + (by + depth), depth)] = part[...]
    for z in range(0, depth, 2):
        for s in range(2):
            pair = [held[z + i, :, s * share : (s + 1) * share] for i in range(2)]
            out_ref[:, (s * depth + z) * share : (s * depth + z + 2) * share] = (
                jnp.concatenate(pair, axis=1)
            )


def join_levels(parts, level):
    depth = len(parts)
    rows, wide = parts[0].shape
    whole = pl.BlockSpec(memory_space=pltpu.VMEM)
    return pl.pallas_call(
        join_kernel,
        out_shape=jax.ShapeDtypeStruct((rows, depth * wide), parts[0].dtype),
        in_specs=[pl.BlockSpec(memory_space=pltpu.SMEM)] + [whole] * depth,
        out_specs=whole,
        scratch_shapes=[pltpu.VMEM((depth, rows, wide), parts[0].dtype)],
        compiler_params=pltpu.CompilerParams(vmem_limit_bytes=40 << 20),
        cost_estimate=pl.CostEstimate(
            flops=0, bytes_accessed=4 * rows * depth * wide, transcendentals=0
        ),
    )(level, *parts)


def pass_on(next_ref, passed_ref):
    for i in range(next_ref.shape[0]):
        passed_ref[i] = next_ref[i]


def mate_kernel(place_ref, core_ref, next_ref, codes_ref, scales_ref, *refs):
    rows_refs, out_ref, passed_ref = refs[:-2], refs[-2], refs[-1]
    pass_on(next_ref, passed_ref)
    values = jnp.concatenate([ref[0, 0] for ref in rows_refs])
    out_ref[...] = scales_ref[...] * jnp.dot(
        values, codes_ref[...], preferred_element_type=jnp.float32
    )


def own_kernel(place_ref, core_ref, next_ref, codes_ref, scales_ref, *refs):
    rows_refs, mate_ref, out_ref, passed_ref = refs[:-3], refs[-3], refs[-2], refs[-1]
    pass_on(next_ref, passed_ref)
    values = jnp.concatenate([ref[0, 0] for ref in rows_refs])
    total = mate_ref[...] + scales_ref[...] * jnp.dot(
        values, codes_ref[...], preferred_element_type=jnp.float32
    )
    places, steps, slots, wide = out_ref.shape
    total = total.reshape(steps, places, slots, wide).astype(out_ref.dtype)
    for step in range(steps):
        out_ref[:, step] = total[step]


def partials(where, core, then, values, codes, scales, mate=None, places=None):
    steps = where.shape[0]
    _, _, rows, half = values.shape
    wide = codes.shape[1]
    flip = 1 if mate is None else 0

    def rows_spec(j):
        return pl.BlockSpec((1, 1, rows, half), lambda i, w, c: (w[j], c[0] ^ flip, 0, 0))

    def whole(*shape):
        return pl.BlockSpec(shape, lambda i, w, c: (0,) * len(shape))

    words = pl.BlockSpec(memory_space=pltpu.SMEM)
    in_specs = [words, whole(half, wide), whole(1, wide)] + [rows_spec(j) for j in range(steps)]
    if mate is None:
        kernel, shape, dtype, extra = mate_kernel, (steps * rows, wide), jnp.float32, ()
    else:
        kernel, extra = own_kernel, (mate,)
        in_specs.append(whole(steps * rows, wide))
        shape, dtype = (places, steps, rows // places, wide), jnp.bfloat16
    return pl.pallas_call(
        kernel,
        out_shape=[jax.ShapeDtypeStruct(shape, dtype), jax.ShapeDtypeStruct(then.shape, then.dtype)],
        grid_spec=pltpu.PrefetchScalarGridSpec(
            num_scalar_prefetch=2, grid=(1,), in_specs=in_specs, out_specs=[whole(*shape), words]
        ),
        compiler_params=pltpu.CompilerParams(vmem_limit_bytes=(58 if mate is None else 40) << 20),
        cost_estimate=pl.CostEstimate(
            flops=2 * steps * rows * half * wide,
            bytes_accessed=steps * rows * (2 * half + 8 * wide),
            transcendentals=0,
        ),
    )(where, core, then, codes, scales, *[values] * steps, *extra)


def weight_kernel(core_ref, values_ref, own_ref, mate_ref, out_ref):
    me = core_ref[0]
    levels = range(values_ref.shape[0])
    rows = [values_ref[z, me] for z in levels] + [values_ref[z, 1 - me] for z in levels]
    units = jnp.concatenate([own_ref[...], mate_ref[...]])
    part = lax.dot_general(
        units, jnp.concatenate(rows), (((0,), (0,)), ((), ())), preferred_element_type=jnp.float32
    )

    @pl.when(pl.program_id(0) == 0)
    def _():
        out_ref[...] = part

    @pl.when(pl.program_id(0) > 0)
    def _():
        out_ref[...] += part


def weight_sums(core, values, own, mate, levels=2):
    depth, _, rows, half = values.shape
    wide = own.shape[1]
    units = pl.BlockSpec((levels * rows, wide), lambda i, c: (i, 0))
    return pl.pallas_call(
        weight_kernel,
        out_shape=jax.ShapeDtypeStruct((wide, half), jnp.float32),
        grid_spec=pltpu.PrefetchScalarGridSpec(
            num_scalar_prefetch=1,
            grid=(depth // levels,),
            in_specs=[
                pl.BlockSpec((levels, 2, rows, half), lambda i, c: (i, 0, 0, 0)), units, units
            ],
            out_specs=pl.BlockSpec((wide, half), lambda i, c: (0, 0)),
        ),
        compiler_params=pltpu.CompilerParams(vmem_limit_bytes=40 << 20),
        cost_estimate=pl.CostEstimate(
            flops=4 * depth * rows * half * wide,
            bytes_accessed=4 * depth * rows * (half + wide) + 4 * half * wide,
            transcendentals=0,
        ),
    )(core, values, own, mate)


def pack_kernel(level_ref, hot_ref, *refs):
    blocks, out_ref = refs[:-1], refs[-1]
    experts, depth, slots, wide = out_ref.shape
    for i, by in enumerate(distances(depth)):
        packed = jnp.dot(hot_ref[i], blocks[i][...], preferred_element_type=jnp.float32)
        level = lax.rem(level_ref[0] + (by + depth), depth)
        out_ref[:, level] = packed.reshape(experts, slots, wide).astype(out_ref.dtype)


def pack_hidden(hot, blocks, level, experts):
    depth, places, rows = hot.shape
    wide = blocks[0].shape[1]
    whole = pl.BlockSpec(memory_space=pltpu.VMEM)
    return pl.pallas_call(
        pack_kernel,
        out_shape=jax.ShapeDtypeStruct((experts, depth, places // experts, wide), jnp.bfloat16),
        in_specs=[pl.BlockSpec(memory_space=pltpu.SMEM)] + [whole] * (depth + 1),
        out_specs=whole,
        compiler_params=pltpu.CompilerParams(vmem_limit_bytes=32 << 20),
        cost_estimate=pl.CostEstimate(
            flops=2 * depth * places * rows * wide,
            bytes_accessed=2 * depth * (places + rows) * wide,
            transcendentals=0,
        ),
    )(level, hot, *blocks)


def shards(cotangent, hidden, codes, scales, counts):
    rows, cols = cotangent.shape
    half = cols // 2
    share = codes.shape[1]
    places = lax.axis_size(PLACES)
    depth = lax.axis_size("z")
    experts = counts.shape[1]
    slots = 3 * rows // (2 * experts)
    wide = 2 * share
    order = distances(depth)
    place, core = lax.axis_index(PLACES), lax.axis_index("c")
    side, level = lax.axis_index("xl"), lax.axis_index("z")
    core_word = core.astype(jnp.int32).reshape(1)
    level_word = level.astype(jnp.int32).reshape(1)

    def levels_at(steps):
        return (level.astype(jnp.int32) + jnp.array(steps, jnp.int32) + depth) % depth

    table = counts.reshape(places, 2, 2, depth, experts)
    line_counts = lax.dynamic_slice(
        table, (place, core, side, 0, 0), (1, 1, 1, depth, experts)
    ).reshape(depth, experts)
    near_counts = lax.dynamic_slice_in_dim(jnp.concatenate([line_counts] * 2), level, depth, 0)
    near_counts = jnp.stack([near_counts[by % depth] for by in order])
    near_hot = slot_hot(near_counts, slots, rows)
    own_hot = near_hot[-1].reshape(experts * slots, rows)

    other_codes, other_scales = lax.ppermute((codes[0], scales[0]), "xl", SWAP)
    by_level = split_levels(hidden, level_word, depth)

    packed = jnp.stack(
        [
            jnp.dot(own_hot, cotangent[:, c * half : (c + 1) * half],
                    preferred_element_type=jnp.float32).astype(jnp.bfloat16)
            for c in range(2)
        ]
    ).reshape(2 * experts, slots, half)
    arrived = lax.all_to_all(packed, ("c",) + PLACES, 0, 0).reshape(2, places * slots, half)

    line_hidden = {}
    for block, by in zip(by_level, order):
        line_hidden[-by if by < depth // 2 else by] = along_z(block, by) if by else block
    arrived, line_hidden[-1], line_hidden[1] = lax.optimization_barrier(
        (arrived, line_hidden[-1], line_hidden[1])
    )
    values = lax.all_gather(arrived.reshape(2 * places * slots, half), "z", axis=0, tiled=True)
    values = values.reshape(depth, 2, places * slots, half)

    first = side == 0
    both_codes = jnp.where(first, jnp.stack([codes[0], other_codes]),
                           jnp.stack([other_codes, codes[0]])).reshape(wide, half).T
    both_scales = jnp.where(first, jnp.stack([scales[0], other_scales]),
                            jnp.stack([other_scales, scales[0]])).reshape(1, wide)
    both_codes, both_scales, *line_hidden = lax.optimization_barrier(
        [both_codes, both_scales] + [line_hidden[by] for by in order]
    )

    hidden_slots = pack_hidden(
        near_hot.reshape(depth, experts * slots, rows), line_hidden, level_word, experts
    )
    own_hidden = lax.all_to_all(hidden_slots, PLACES, 0, 0)
    own_hidden = own_hidden.transpose(1, 0, 2, 3).reshape(depth * places * slots, wide)
    mate_hidden = lax.ppermute(own_hidden, "c", SWAP)
    values = after(values, own_hidden)

    def product(where, then, *mate):
        args = (where, core_word, then, values, both_codes, both_scales)
        return partials(*args, *mate, places) if mate else partials(*args)

    def unpack(hot, back):
        return jnp.einsum("zesr,ezsw->zrw", hot, back,
                          preferred_element_type=jnp.float32).astype(jnp.bfloat16)

    came = {}

    def send_home(steps, back):
        blocks = lax.optimization_barrier([back[i] for i in range(len(steps))])
        for by, block in zip(steps, blocks):
            came[-by if by < depth // 2 else by] = along_z(block, by) if by else block
        return blocks

    cut = 3
    far_at, close_at = levels_at(order[:cut]), levels_at(order[cut:])
    far_mate, far_at = product(far_at, far_at)
    far_joined, close_at = product(far_at, close_at, lax.ppermute(far_mate, "c", SWAP))
    close_mate, close_at = product(close_at, close_at)
    close_joined, _ = product(close_at, far_at, lax.ppermute(close_mate, "c", SWAP))
    far_raw = after(lax.all_to_all(far_joined, PLACES, 0, 0), close_joined)
    far_back = send_home(order[:cut], unpack(near_hot[:cut], far_raw))
    close_raw = after(lax.all_to_all(close_joined, PLACES, 0, 0), *came.values())
    send_home(order[cut:], unpack(near_hot[cut:], close_raw))

    own_hidden, mate_hidden = after((own_hidden, mate_hidden), *far_back)
    sums = weight_sums(core_word, values, own_hidden, mate_hidden).reshape(2, share, half)
    gone = lax.dynamic_index_in_dim(sums, 1 - side, 0, keepdims=False)
    kept = lax.dynamic_index_in_dim(sums, side, 0, keepdims=False)
    largest = jnp.maximum(jnp.max(jnp.abs(gone)), 1e-30).reshape(1)
    gone = (gone * (1 / largest)).astype(jnp.float16)
    largest = lax.ppermute(largest, "xl", SWAP)
    gone, kept, largest, _ = lax.optimization_barrier((gone, kept, largest, close_raw))
    gone = lax.ppermute(gone, "xl", SWAP)
    weight_grad = kept + gone.astype(jnp.float32) * largest
    d_hidden = join_levels([came[by] for by in order], after(level_word, weight_grad))
    return d_hidden, weight_grad[None]


def solution(mesh):
    lanes, lines = mesh.devices.shape
    fine = Mesh(mesh.devices.reshape(2, lanes // 4, 2, 2, lines // 2), ("xh", "y", "c", "xl", "z"))
    expert, dp = ("xh", "y", "c"), ("xl", "z")
    in_specs = (P(expert + dp, None), P(expert + dp, None), P(expert, dp, None), P(expert, dp), P())
    out_specs = (P(expert + dp, None), P(expert, dp, None))
    return jax.shard_map(shards, mesh=fine, in_specs=in_specs, out_specs=out_specs, check_vma=False)
```

```python
import jax
import jax.numpy as jnp
from jax import lax
from jax.experimental import pallas as pl
from jax.experimental.pallas import tpu as pltpu
from jax.sharding import Mesh, PartitionSpec as P

PLACES = ("xh", "y")
SWAP = [(0, 1), (1, 0)]


def slot_hot(row_counts, slots, rows):
    starts = jnp.cumsum(row_counts, axis=-1) - row_counts
    slot = jnp.arange(slots, dtype=jnp.int32)
    source = jnp.where(slot < row_counts[..., None], starts[..., None] + slot, -1)
    return (source[..., None] == jnp.arange(rows, dtype=jnp.int32)).astype(jnp.bfloat16)


def distances(depth):
    order = [depth // 2]
    for k in range(depth // 2 - 1, 0, -1):
        order += [k, -k]
    return order + [0]


def after(value, *others):
    return lax.optimization_barrier((value,) + others)[0]


def along_z(value, by):
    depth = lax.axis_size("z")
    return lax.ppermute(value, "z", [(i, (i + by) % depth) for i in range(depth)])


def split_kernel(level_ref, hidden_ref, *refs):
    outs, held = refs[:-1], refs[-1]
    depth, _, wide = held.shape
    share = wide // 2
    for z in range(depth):
        low = hidden_ref[:, z * share : (z + 1) * share]
        high = hidden_ref[:, (depth + z) * share : (depth + z + 1) * share]
        held[z] = jnp.concatenate([low, high], axis=1)
    for out, by in zip(outs, distances(depth)):
        out[...] = held[lax.rem(level_ref[0] + (by + depth), depth)]


def split_levels(hidden, level, depth):
    rows, width = hidden.shape
    block = (rows, width // depth)
    whole = pl.BlockSpec(memory_space=pltpu.VMEM)
    return pl.pallas_call(
        split_kernel,
        out_shape=[jax.ShapeDtypeStruct(block, hidden.dtype)] * depth,
        in_specs=[pl.BlockSpec(memory_space=pltpu.SMEM), whole],
        out_specs=[whole] * depth,
        scratch_shapes=[pltpu.VMEM((depth,) + block, hidden.dtype)],
        compiler_params=pltpu.CompilerParams(vmem_limit_bytes=40 << 20),
    )(level, hidden)


def join_kernel(level_ref, *refs):
    parts, out_ref, held = refs[:-2], refs[-2], refs[-1]
    depth, _, wide = held.shape
    share = wide // 2
    for part, by in zip(parts, distances(depth)):
        held[lax.rem(level_ref[0] + (by + depth), depth)] = part[...]
    for z in range(0, depth, 2):
        for s in range(2):
            pair = [held[z + i, :, s * share : (s + 1) * share] for i in range(2)]
            out_ref[:, (s * depth + z) * share : (s * depth + z + 2) * share] = (
                jnp.concatenate(pair, axis=1)
            )


def join_levels(parts, level):
    depth = len(parts)
    rows, wide = parts[0].shape
    whole = pl.BlockSpec(memory_space=pltpu.VMEM)
    return pl.pallas_call(
        join_kernel,
        out_shape=jax.ShapeDtypeStruct((rows, depth * wide), parts[0].dtype),
        in_specs=[pl.BlockSpec(memory_space=pltpu.SMEM)] + [whole] * depth,
        out_specs=whole,
        scratch_shapes=[pltpu.VMEM((depth, rows, wide), parts[0].dtype)],
        compiler_params=pltpu.CompilerParams(vmem_limit_bytes=40 << 20),
    )(level, *parts)


def pass_on(next_ref, passed_ref):
    for i in range(next_ref.shape[0]):
        passed_ref[i] = next_ref[i]


def mate_kernel(place_ref, core_ref, next_ref, codes_ref, scales_ref, *refs):
    rows_refs, out_ref, passed_ref = refs[:-2], refs[-2], refs[-1]
    pass_on(next_ref, passed_ref)
    values = jnp.concatenate([ref[0, 0] for ref in rows_refs])
    out_ref[...] = scales_ref[...] * jnp.dot(
        values, codes_ref[...], preferred_element_type=jnp.float32
    )


def own_kernel(place_ref, core_ref, next_ref, codes_ref, scales_ref, *refs):
    rows_refs, mate_ref, out_ref, passed_ref = refs[:-3], refs[-3], refs[-2], refs[-1]
    pass_on(next_ref, passed_ref)
    values = jnp.concatenate([ref[0, 0] for ref in rows_refs])
    total = mate_ref[...] + scales_ref[...] * jnp.dot(
        values, codes_ref[...], preferred_element_type=jnp.float32
    )
    places, steps, slots, wide = out_ref.shape
    total = total.reshape(steps, places, slots, wide).astype(out_ref.dtype)
    for step in range(steps):
        out_ref[:, step] = total[step]


def partials(where, core, then, values, codes, scales, mate=None, places=None):
    steps = where.shape[0]
    _, _, rows, half = values.shape
    wide = codes.shape[1]
    flip = 1 if mate is None else 0

    def rows_spec(j):
        return pl.BlockSpec((1, 1, rows, half), lambda i, w, c: (w[j], c[0] ^ flip, 0, 0))

    def whole(*shape):
        return pl.BlockSpec(shape, lambda i, w, c: (0,) * len(shape))

    words = pl.BlockSpec(memory_space=pltpu.SMEM)
    in_specs = [words, whole(half, wide), whole(1, wide)] + [rows_spec(j) for j in range(steps)]
    if mate is None:
        kernel, shape, dtype, extra = mate_kernel, (steps * rows, wide), jnp.float32, ()
    else:
        kernel, extra = own_kernel, (mate,)
        in_specs.append(whole(steps * rows, wide))
        shape, dtype = (places, steps, rows // places, wide), jnp.bfloat16
    return pl.pallas_call(
        kernel,
        out_shape=[jax.ShapeDtypeStruct(shape, dtype), jax.ShapeDtypeStruct(then.shape, then.dtype)],
        grid_spec=pltpu.PrefetchScalarGridSpec(
            num_scalar_prefetch=2, grid=(1,), in_specs=in_specs, out_specs=[whole(*shape), words]
        ),
        compiler_params=pltpu.CompilerParams(vmem_limit_bytes=40 << 20),
    )(where, core, then, codes, scales, *[values] * steps, *extra)


def weight_kernel(core_ref, values_ref, own_ref, mate_ref, out_ref):
    me = core_ref[0]
    levels = range(values_ref.shape[0])
    rows = [values_ref[z, me] for z in levels] + [values_ref[z, 1 - me] for z in levels]
    units = jnp.concatenate([own_ref[...], mate_ref[...]])
    part = lax.dot_general(
        units, jnp.concatenate(rows), (((0,), (0,)), ((), ())), preferred_element_type=jnp.float32
    )

    @pl.when(pl.program_id(0) == 0)
    def _():
        out_ref[...] = part

    @pl.when(pl.program_id(0) > 0)
    def _():
        out_ref[...] += part


def weight_sums(core, values, own, mate, levels=2):
    depth, _, rows, half = values.shape
    wide = own.shape[1]
    units = pl.BlockSpec((levels * rows, wide), lambda i, c: (i, 0))
    return pl.pallas_call(
        weight_kernel,
        out_shape=jax.ShapeDtypeStruct((wide, half), jnp.float32),
        grid_spec=pltpu.PrefetchScalarGridSpec(
            num_scalar_prefetch=1,
            grid=(depth // levels,),
            in_specs=[
                pl.BlockSpec((levels, 2, rows, half), lambda i, c: (i, 0, 0, 0)), units, units
            ],
            out_specs=pl.BlockSpec((wide, half), lambda i, c: (0, 0)),
        ),
        compiler_params=pltpu.CompilerParams(vmem_limit_bytes=40 << 20),
    )(core, values, own, mate)


def rows_kernel(counts_ref, rows_ref, out_ref):
    halves, experts, slots, half = out_ref.shape
    rows = rows_ref.shape[0]
    slot = lax.broadcasted_iota(jnp.int32, (slots, rows), 0)
    row = lax.broadcasted_iota(jnp.int32, (slots, rows), 1)
    hot, start = [], 0
    for e in range(experts):
        count = counts_ref[e]
        hit = jnp.logical_and(row == slot + start, slot < count)
        hot.append(jnp.where(hit, 1.0, 0.0))
        start = start + count
    hot = jnp.concatenate(hot).astype(jnp.bfloat16)
    for c in range(halves):
        packed = jnp.dot(
            hot, rows_ref[:, c * half : (c + 1) * half], preferred_element_type=jnp.float32
        )
        out_ref[c] = packed.reshape(experts, slots, half).astype(out_ref.dtype)


def pack_rows(counts, cotangent, slots):
    rows, cols = cotangent.shape
    whole = pl.BlockSpec(memory_space=pltpu.VMEM)
    return pl.pallas_call(
        rows_kernel,
        out_shape=jax.ShapeDtypeStruct((2, counts.shape[0], slots, cols // 2), cotangent.dtype),
        in_specs=[pl.BlockSpec(memory_space=pltpu.SMEM), whole],
        out_specs=whole,
        compiler_params=pltpu.CompilerParams(vmem_limit_bytes=40 << 20),
    )(counts, cotangent)


def unpack_kernel(hot_ref, back_ref, *outs):
    experts, _, slots, wide = back_ref.shape
    for i, out in enumerate(outs):
        packed = back_ref[:, i].astype(jnp.float32).reshape(experts * slots, wide)
        out[...] = lax.dot_general(
            hot_ref[i], packed.astype(jnp.bfloat16), (((0,), (0,)), ((), ())),
            preferred_element_type=jnp.float32,
        ).astype(out.dtype)


def unpack(hot, back):
    steps, _, rows = hot.shape
    whole = pl.BlockSpec(memory_space=pltpu.VMEM)
    return pl.pallas_call(
        unpack_kernel,
        out_shape=[jax.ShapeDtypeStruct((rows, back.shape[-1]), back.dtype)] * steps,
        in_specs=[whole, whole],
        out_specs=[whole] * steps,
        compiler_params=pltpu.CompilerParams(vmem_limit_bytes=40 << 20),
    )(hot, back)


def pack_kernel(level_ref, hot_ref, *refs):
    blocks, out_ref = refs[:-1], refs[-1]
    experts, depth, slots, wide = out_ref.shape
    for i, by in enumerate(distances(depth)):
        packed = jnp.dot(hot_ref[i], blocks[i][...], preferred_element_type=jnp.float32)
        level = lax.rem(level_ref[0] + (by + depth), depth)
        out_ref[:, level] = packed.reshape(experts, slots, wide).astype(out_ref.dtype)


def pack_hidden(hot, blocks, level, experts):
    depth, places, rows = hot.shape
    wide = blocks[0].shape[1]
    whole = pl.BlockSpec(memory_space=pltpu.VMEM)
    return pl.pallas_call(
        pack_kernel,
        out_shape=jax.ShapeDtypeStruct((experts, depth, places // experts, wide), jnp.bfloat16),
        in_specs=[pl.BlockSpec(memory_space=pltpu.SMEM)] + [whole] * (depth + 1),
        out_specs=whole,
        compiler_params=pltpu.CompilerParams(vmem_limit_bytes=40 << 20),
    )(level, hot, *blocks)


def shards(cotangent, hidden, codes, scales, counts):
    rows, cols = cotangent.shape
    half = cols // 2
    share = codes.shape[1]
    places = lax.axis_size(PLACES)
    depth = lax.axis_size("z")
    experts = counts.shape[1]
    slots = 3 * rows // (2 * experts)
    wide = 2 * share
    order = distances(depth)
    place, core = lax.axis_index(PLACES), lax.axis_index("c")
    side, level = lax.axis_index("xl"), lax.axis_index("z")
    core_word = core.astype(jnp.int32).reshape(1)
    level_word = level.astype(jnp.int32).reshape(1)

    def levels_at(steps):
        return (level.astype(jnp.int32) + jnp.array(steps, jnp.int32) + depth) % depth

    line_at = ((place * 2 + core) * 2 + side) * depth
    own_counts = lax.dynamic_slice_in_dim(counts, line_at + level, 1, 0).reshape(experts)
    line_counts = lax.dynamic_slice_in_dim(counts, line_at, depth, 0)
    near_counts = lax.dynamic_slice_in_dim(jnp.concatenate([line_counts] * 2), level, depth, 0)
    near_counts = jnp.stack([near_counts[by % depth] for by in order])
    near_hot = slot_hot(near_counts, slots, rows).reshape(depth, experts * slots, rows)

    other_codes, other_scales = lax.ppermute((codes[0], scales[0]), "xl", SWAP)
    by_level = split_levels(hidden, level_word, depth)

    packed = pack_rows(own_counts, cotangent, slots).reshape(2 * experts, slots, half)
    arrived = lax.all_to_all(packed, ("c",) + PLACES, 0, 0).reshape(2, places * slots, half)

    line_hidden = {}
    for block, by in zip(by_level, order):
        line_hidden[-by if by < depth // 2 else by] = along_z(block, by) if by else block
    arrived, line_hidden[-1], line_hidden[1] = lax.optimization_barrier(
        (arrived, line_hidden[-1], line_hidden[1])
    )
    values = lax.all_gather(arrived.reshape(2 * places * slots, half), "z", axis=0, tiled=True)
    values = values.reshape(depth, 2, places * slots, half)

    first = side == 0
    both_codes = jnp.where(first, jnp.stack([codes[0], other_codes]),
                           jnp.stack([other_codes, codes[0]])).reshape(wide, half).T
    both_scales = jnp.where(first, jnp.stack([scales[0], other_scales]),
                            jnp.stack([other_scales, scales[0]])).reshape(1, wide)
    both_codes, both_scales, *line_hidden = lax.optimization_barrier(
        [both_codes, both_scales] + [line_hidden[by] for by in order]
    )

    hidden_slots = pack_hidden(near_hot, line_hidden, level_word, experts)
    own_hidden = lax.all_to_all(hidden_slots, PLACES, 0, 0)
    own_hidden = own_hidden.transpose(1, 0, 2, 3).reshape(depth * places * slots, wide)
    mate_hidden = lax.ppermute(own_hidden, "c", SWAP)
    values = after(values, own_hidden)

    def product(where, then, *mate):
        args = (where, core_word, then, values, both_codes, both_scales)
        return partials(*args, *mate, places) if mate else partials(*args)

    came = {}

    def send_home(steps, back):
        for by, block in zip(steps, back):
            came[-by if by < depth // 2 else by] = along_z(block, by) if by else block

    cut = 3
    far_at, close_at = levels_at(order[:cut]), levels_at(order[cut:])
    far_mate, far_at = product(far_at, far_at)
    far_joined, close_at = product(far_at, close_at, lax.ppermute(far_mate, "c", SWAP))
    close_mate, close_at = product(close_at, close_at)
    close_joined, _ = product(close_at, far_at, lax.ppermute(close_mate, "c", SWAP))
    sums = weight_sums(core_word, values, own_hidden, mate_hidden)
    close_joined = after(close_joined, sums)
    far_raw = after(lax.all_to_all(far_joined, PLACES, 0, 0), close_joined, sums)
    send_home(order[:cut], unpack(near_hot[:cut], far_raw))
    close_raw = after(lax.all_to_all(close_joined, PLACES, 0, 0), *came.values())
    send_home(order[cut:], unpack(near_hot[cut:], close_raw))

    sums = sums.reshape(2, share, half)
    gone = lax.dynamic_index_in_dim(sums, 1 - side, 0, keepdims=False)
    kept = lax.dynamic_index_in_dim(sums, side, 0, keepdims=False)
    largest = jnp.maximum(jnp.max(jnp.abs(gone)), 1e-30).reshape(1)
    gone = (gone * (1 / largest)).astype(jnp.float16)
    largest = lax.ppermute(largest, "xl", SWAP)
    gone, kept, largest, _ = lax.optimization_barrier((gone, kept, largest, close_raw))
    gone = lax.ppermute(gone, "xl", SWAP)
    weight_grad = kept + gone.astype(jnp.float32) * largest
    d_hidden = join_levels([came[by] for by in order], after(level_word, weight_grad))
    return d_hidden, weight_grad[None]


def solution(mesh):
    lanes, lines = mesh.devices.shape
    fine = Mesh(mesh.devices.reshape(2, lanes // 4, 2, 2, lines // 2), ("xh", "y", "c", "xl", "z"))
    expert, dp = ("xh", "y", "c"), ("xl", "z")
    in_specs = (P(expert + dp, None), P(expert + dp, None), P(expert, dp, None), P(expert, dp), P())
    out_specs = (P(expert + dp, None), P(expert, dp, None))
    return jax.shard_map(shards, mesh=fine, in_specs=in_specs, out_specs=out_specs, check_vma=False)
```

```python
import jax
import jax.numpy as jnp
from jax import lax
from jax.experimental import pallas as pl
from jax.experimental.pallas import tpu as pltpu
from jax.sharding import Mesh, PartitionSpec as P

PLACES = ("xh", "y")
SWAP = [(0, 1), (1, 0)]


def slot_hot(row_counts, slots, rows):
    starts = jnp.cumsum(row_counts, axis=-1) - row_counts
    slot = jnp.arange(slots, dtype=jnp.int32)
    source = jnp.where(slot < row_counts[..., None], starts[..., None] + slot, -1)
    return (source[..., None] == jnp.arange(rows, dtype=jnp.int32)).astype(jnp.bfloat16)


def distances(depth):
    order = [depth // 2]
    for k in range(depth // 2 - 1, 0, -1):
        order += [k, -k]
    return order + [0]


def after(value, *others):
    return lax.optimization_barrier((value,) + others)[0]


def along_z(value, by):
    depth = lax.axis_size("z")
    return lax.ppermute(value, "z", [(i, (i + by) % depth) for i in range(depth)])


def split_kernel(level_ref, hidden_ref, *refs):
    outs, held = refs[:-1], refs[-1]
    depth, _, wide = held.shape
    share = wide // 2
    for z in range(depth):
        low = hidden_ref[:, z * share : (z + 1) * share]
        high = hidden_ref[:, (depth + z) * share : (depth + z + 1) * share]
        held[z] = jnp.concatenate([low, high], axis=1)
    for out, by in zip(outs, distances(depth)):
        out[...] = held[lax.rem(level_ref[0] + (by + depth), depth)]


def split_levels(hidden, level, depth):
    rows, width = hidden.shape
    block = (rows, width // depth)
    whole = pl.BlockSpec(memory_space=pltpu.VMEM)
    return pl.pallas_call(
        split_kernel,
        out_shape=[jax.ShapeDtypeStruct(block, hidden.dtype)] * depth,
        in_specs=[pl.BlockSpec(memory_space=pltpu.SMEM), whole],
        out_specs=[whole] * depth,
        scratch_shapes=[pltpu.VMEM((depth,) + block, hidden.dtype)],
        compiler_params=pltpu.CompilerParams(vmem_limit_bytes=40 << 20),
    )(level, hidden)


def join_kernel(level_ref, *refs):
    parts, out_ref, held = refs[:-2], refs[-2], refs[-1]
    depth, _, wide = held.shape
    share = wide // 2
    for part, by in zip(parts, distances(depth)):
        held[lax.rem(level_ref[0] + (by + depth), depth)] = part[...]
    for z in range(0, depth, 2):
        for s in range(2):
            pair = [held[z + i, :, s * share : (s + 1) * share] for i in range(2)]
            out_ref[:, (s * depth + z) * share : (s * depth + z + 2) * share] = (
                jnp.concatenate(pair, axis=1)
            )


def join_levels(parts, level):
    depth = len(parts)
    rows, wide = parts[0].shape
    whole = pl.BlockSpec(memory_space=pltpu.VMEM)
    return pl.pallas_call(
        join_kernel,
        out_shape=jax.ShapeDtypeStruct((rows, depth * wide), parts[0].dtype),
        in_specs=[pl.BlockSpec(memory_space=pltpu.SMEM)] + [whole] * depth,
        out_specs=whole,
        scratch_shapes=[pltpu.VMEM((depth, rows, wide), parts[0].dtype)],
        compiler_params=pltpu.CompilerParams(vmem_limit_bytes=40 << 20),
    )(level, *parts)


def pass_on(next_ref, passed_ref):
    for i in range(next_ref.shape[0]):
        passed_ref[i] = next_ref[i]


def mate_kernel(place_ref, core_ref, next_ref, codes_ref, scales_ref, *refs):
    rows_refs, out_ref, passed_ref = refs[:-2], refs[-2], refs[-1]
    pass_on(next_ref, passed_ref)
    values = jnp.concatenate([ref[0, 0] for ref in rows_refs])
    out_ref[...] = scales_ref[...] * jnp.dot(
        values, codes_ref[...], preferred_element_type=jnp.float32
    )


def own_kernel(place_ref, core_ref, next_ref, codes_ref, scales_ref, *refs):
    rows_refs, mate_ref, out_ref, passed_ref = refs[:-3], refs[-3], refs[-2], refs[-1]
    pass_on(next_ref, passed_ref)
    values = jnp.concatenate([ref[0, 0] for ref in rows_refs])
    total = mate_ref[...] + scales_ref[...] * jnp.dot(
        values, codes_ref[...], preferred_element_type=jnp.float32
    )
    places, steps, slots, wide = out_ref.shape
    total = total.reshape(steps, places, slots, wide).astype(out_ref.dtype)
    for step in range(steps):
        out_ref[:, step] = total[step]


def partials(where, core, then, values, codes, scales, mate=None, places=None):
    steps = where.shape[0]
    _, _, rows, half = values.shape
    wide = codes.shape[1]
    flip = 1 if mate is None else 0

    def rows_spec(j):
        return pl.BlockSpec((1, 1, rows, half), lambda i, w, c: (w[j], c[0] ^ flip, 0, 0))

    def whole(*shape):
        return pl.BlockSpec(shape, lambda i, w, c: (0,) * len(shape))

    words = pl.BlockSpec(memory_space=pltpu.SMEM)
    in_specs = [words, whole(half, wide), whole(1, wide)] + [rows_spec(j) for j in range(steps)]
    if mate is None:
        kernel, shape, dtype, extra = mate_kernel, (steps * rows, wide), jnp.float32, ()
        place = jax.ShapeDtypeStruct
    else:
        kernel, extra, place = own_kernel, (mate,), pltpu.HBM
        in_specs.append(whole(steps * rows, wide))
        shape, dtype = (places, steps, rows // places, wide), jnp.bfloat16
    return pl.pallas_call(
        kernel,
        out_shape=[place(shape, dtype), jax.ShapeDtypeStruct(then.shape, then.dtype)],
        grid_spec=pltpu.PrefetchScalarGridSpec(
            num_scalar_prefetch=2, grid=(1,), in_specs=in_specs, out_specs=[whole(*shape), words]
        ),
        compiler_params=pltpu.CompilerParams(vmem_limit_bytes=40 << 20),
    )(where, core, then, codes, scales, *[values] * steps, *extra)


def weight_kernel(core_ref, values_ref, own_ref, mate_ref, out_ref):
    me = core_ref[0]
    levels = range(values_ref.shape[0])
    rows = [values_ref[z, me] for z in levels] + [values_ref[z, 1 - me] for z in levels]
    units = jnp.concatenate([own_ref[...], mate_ref[...]])
    part = lax.dot_general(
        units, jnp.concatenate(rows), (((0,), (0,)), ((), ())), preferred_element_type=jnp.float32
    )

    @pl.when(pl.program_id(0) == 0)
    def _():
        out_ref[...] = part

    @pl.when(pl.program_id(0) > 0)
    def _():
        out_ref[...] += part


def weight_sums(core, values, own, mate, levels=2):
    depth, _, rows, half = values.shape
    wide = own.shape[1]
    units = pl.BlockSpec((levels * rows, wide), lambda i, c: (i, 0))
    return pl.pallas_call(
        weight_kernel,
        out_shape=pltpu.HBM((wide, half), jnp.float32),
        grid_spec=pltpu.PrefetchScalarGridSpec(
            num_scalar_prefetch=1,
            grid=(depth // levels,),
            in_specs=[
                pl.BlockSpec((levels, 2, rows, half), lambda i, c: (i, 0, 0, 0)), units, units
            ],
            out_specs=pl.BlockSpec((wide, half), lambda i, c: (0, 0)),
        ),
        compiler_params=pltpu.CompilerParams(vmem_limit_bytes=40 << 20),
    )(core, values, own, mate)


def rows_kernel(counts_ref, rows_ref, out_ref):
    halves, experts, slots, half = out_ref.shape
    rows = rows_ref.shape[0]
    slot = lax.broadcasted_iota(jnp.int32, (slots, rows), 0)
    row = lax.broadcasted_iota(jnp.int32, (slots, rows), 1)
    hot, start = [], 0
    for e in range(experts):
        count = counts_ref[e]
        hit = jnp.logical_and(row == slot + start, slot < count)
        hot.append(jnp.where(hit, 1.0, 0.0))
        start = start + count
    hot = jnp.concatenate(hot).astype(jnp.bfloat16)
    for c in range(halves):
        packed = jnp.dot(
            hot, rows_ref[:, c * half : (c + 1) * half], preferred_element_type=jnp.float32
        )
        out_ref[c] = packed.reshape(experts, slots, half).astype(out_ref.dtype)


def pack_rows(counts, cotangent, slots):
    rows, cols = cotangent.shape
    whole = pl.BlockSpec(memory_space=pltpu.VMEM)
    return pl.pallas_call(
        rows_kernel,
        out_shape=jax.ShapeDtypeStruct((2, counts.shape[0], slots, cols // 2), cotangent.dtype),
        in_specs=[pl.BlockSpec(memory_space=pltpu.SMEM), whole],
        out_specs=whole,
        compiler_params=pltpu.CompilerParams(vmem_limit_bytes=40 << 20),
    )(counts, cotangent)


def unpack_kernel(hot_ref, back_ref, *outs):
    experts, _, slots, wide = back_ref.shape
    for i, out in enumerate(outs):
        packed = back_ref[:, i].astype(jnp.float32).reshape(experts * slots, wide)
        out[...] = lax.dot_general(
            hot_ref[i], packed.astype(jnp.bfloat16), (((0,), (0,)), ((), ())),
            preferred_element_type=jnp.float32,
        ).astype(out.dtype)


def unpack(hot, back):
    steps, _, rows = hot.shape
    whole = pl.BlockSpec(memory_space=pltpu.VMEM)
    return pl.pallas_call(
        unpack_kernel,
        out_shape=[jax.ShapeDtypeStruct((rows, back.shape[-1]), back.dtype)] * steps,
        in_specs=[whole, whole],
        out_specs=[whole] * steps,
        compiler_params=pltpu.CompilerParams(vmem_limit_bytes=40 << 20),
    )(hot, back)


def pack_kernel(level_ref, hot_ref, *refs):
    blocks, out_ref = refs[:-1], refs[-1]
    experts, depth, slots, wide = out_ref.shape
    for i, by in enumerate(distances(depth)):
        packed = jnp.dot(hot_ref[i], blocks[i][...], preferred_element_type=jnp.float32)
        level = lax.rem(level_ref[0] + (by + depth), depth)
        out_ref[:, level] = packed.reshape(experts, slots, wide).astype(out_ref.dtype)


def pack_hidden(hot, blocks, level, experts):
    depth, places, rows = hot.shape
    wide = blocks[0].shape[1]
    whole = pl.BlockSpec(memory_space=pltpu.VMEM)
    return pl.pallas_call(
        pack_kernel,
        out_shape=pltpu.HBM((experts, depth, places // experts, wide), jnp.bfloat16),
        in_specs=[pl.BlockSpec(memory_space=pltpu.SMEM)] + [whole] * (depth + 1),
        out_specs=whole,
        compiler_params=pltpu.CompilerParams(vmem_limit_bytes=40 << 20),
    )(level, hot, *blocks)


def shards(cotangent, hidden, codes, scales, counts):
    rows, cols = cotangent.shape
    half = cols // 2
    share = codes.shape[1]
    places = lax.axis_size(PLACES)
    depth = lax.axis_size("z")
    experts = counts.shape[1]
    slots = 3 * rows // (2 * experts)
    wide = 2 * share
    order = distances(depth)
    place, core = lax.axis_index(PLACES), lax.axis_index("c")
    side, level = lax.axis_index("xl"), lax.axis_index("z")
    core_word = core.astype(jnp.int32).reshape(1)
    level_word = level.astype(jnp.int32).reshape(1)

    def levels_at(steps):
        return (level.astype(jnp.int32) + jnp.array(steps, jnp.int32) + depth) % depth

    line_at = ((place * 2 + core) * 2 + side) * depth
    own_counts = lax.dynamic_slice_in_dim(counts, line_at + level, 1, 0).reshape(experts)
    line_counts = lax.dynamic_slice_in_dim(counts, line_at, depth, 0)
    near_counts = lax.dynamic_slice_in_dim(jnp.concatenate([line_counts] * 2), level, depth, 0)
    near_counts = jnp.stack([near_counts[by % depth] for by in order])
    near_hot = slot_hot(near_counts, slots, rows).reshape(depth, experts * slots, rows)

    other_codes, other_scales = lax.ppermute((codes[0], scales[0]), "xl", SWAP)
    by_level = split_levels(hidden, level_word, depth)

    packed = pack_rows(own_counts, cotangent, slots).reshape(2 * experts, slots, half)
    arrived = lax.all_to_all(packed, ("c",) + PLACES, 0, 0).reshape(2, places * slots, half)

    line_hidden = {}
    for block, by in zip(by_level, order):
        line_hidden[-by if by < depth // 2 else by] = along_z(block, by) if by else block
    arrived, line_hidden[-1], line_hidden[1] = lax.optimization_barrier(
        (arrived, line_hidden[-1], line_hidden[1])
    )
    values = lax.all_gather(arrived.reshape(2 * places * slots, half), "z", axis=0, tiled=True)
    values = values.reshape(depth, 2, places * slots, half)

    first = side == 0
    both_codes = jnp.where(first, jnp.stack([codes[0], other_codes]),
                           jnp.stack([other_codes, codes[0]])).reshape(wide, half).T
    both_scales = jnp.where(first, jnp.stack([scales[0], other_scales]),
                            jnp.stack([other_scales, scales[0]])).reshape(1, wide)
    both_codes, both_scales, *line_hidden = lax.optimization_barrier(
        [both_codes, both_scales] + [line_hidden[by] for by in order]
    )

    hidden_slots = pack_hidden(near_hot, line_hidden, level_word, experts)
    own_hidden = lax.all_to_all(hidden_slots, PLACES, 0, 0)
    own_hidden = own_hidden.transpose(1, 0, 2, 3).reshape(depth * places * slots, wide)
    mate_hidden = lax.ppermute(own_hidden, "c", SWAP)
    values = after(values, own_hidden)

    pinned = pltpu.with_memory_space_constraint(values, pltpu.HBM)

    def product(values, where, then, *mate):
        args = (where, core_word, then, values, both_codes, both_scales)
        return partials(*args, *mate, places) if mate else partials(*args)

    came = {}

    def send_home(steps, back):
        for by, block in zip(steps, back):
            came[-by if by < depth // 2 else by] = along_z(block, by) if by else block

    cut = 3
    far_at, close_at = levels_at(order[:cut]), levels_at(order[cut:])
    far_mate, far_at = product(pinned, far_at, far_at)
    far_joined, close_at = product(values, far_at, close_at, lax.ppermute(far_mate, "c", SWAP))
    close_mate, close_at = product(values, close_at, close_at)
    close_joined, _ = product(pinned, close_at, far_at, lax.ppermute(close_mate, "c", SWAP))
    far_raw = after(lax.all_to_all(far_joined, PLACES, 0, 0), close_joined)
    far_back = unpack(near_hot[:cut], far_raw)
    send_home(order[:cut], far_back)
    close_raw = after(lax.all_to_all(close_joined, PLACES, 0, 0), *came.values())
    send_home(order[cut:], unpack(near_hot[cut:], close_raw))

    own_hidden, mate_hidden = after((own_hidden, mate_hidden), *far_back)
    sums = weight_sums(core_word, pinned, own_hidden, mate_hidden).reshape(2, share, half)
    gone = lax.dynamic_index_in_dim(sums, 1 - side, 0, keepdims=False)
    kept = lax.dynamic_index_in_dim(sums, side, 0, keepdims=False)
    largest = jnp.maximum(jnp.max(jnp.abs(gone)), 1e-30).reshape(1)
    gone = (gone * (1 / largest)).astype(jnp.float16)
    largest = lax.ppermute(largest, "xl", SWAP)
    gone, kept, largest, _ = lax.optimization_barrier((gone, kept, largest, close_raw))
    gone = lax.ppermute(gone, "xl", SWAP)
    weight_grad = kept + gone.astype(jnp.float32) * largest
    d_hidden = join_levels([came[by] for by in order], after(level_word, weight_grad))
    return d_hidden, weight_grad[None]


def solution(mesh):
    lanes, lines = mesh.devices.shape
    fine = Mesh(mesh.devices.reshape(2, lanes // 4, 2, 2, lines // 2), ("xh", "y", "c", "xl", "z"))
    expert, dp = ("xh", "y", "c"), ("xl", "z")
    in_specs = (P(expert + dp, None), P(expert + dp, None), P(expert, dp, None), P(expert, dp), P())
    out_specs = (P(expert + dp, None), P(expert, dp, None))
    return jax.shard_map(shards, mesh=fine, in_specs=in_specs, out_specs=out_specs, check_vma=False)
```

```python
import jax
import jax.numpy as jnp
from jax import lax
from jax.experimental import pallas as pl
from jax.experimental.pallas import tpu as pltpu
from jax.sharding import Mesh, PartitionSpec as P

PLACES = ("xh", "y")
SWAP = [(0, 1), (1, 0)]


def slot_hot(row_counts, slots, rows):
    starts = jnp.cumsum(row_counts, axis=-1) - row_counts
    slot = jnp.arange(slots, dtype=jnp.int32)
    source = jnp.where(slot < row_counts[..., None], starts[..., None] + slot, -1)
    return (source[..., None] == jnp.arange(rows, dtype=jnp.int32)).astype(jnp.bfloat16)


def distances(depth):
    order = [depth // 2]
    for k in range(depth // 2 - 1, 0, -1):
        order += [k, -k]
    return order + [0]


def after(value, *others):
    return lax.optimization_barrier((value,) + others)[0]


def along_z(value, by):
    depth = lax.axis_size("z")
    return lax.ppermute(value, "z", [(i, (i + by) % depth) for i in range(depth)])


def split_kernel(level_ref, hidden_ref, *refs):
    outs, held = refs[:-1], refs[-1]
    depth, _, wide = held.shape
    share = wide // 2
    for z in range(depth):
        low = hidden_ref[:, z * share : (z + 1) * share]
        high = hidden_ref[:, (depth + z) * share : (depth + z + 1) * share]
        held[z] = jnp.concatenate([low, high], axis=1)
    for out, by in zip(outs, distances(depth)):
        out[...] = held[lax.rem(level_ref[0] + (by + depth), depth)]


def split_levels(hidden, level, depth):
    rows, width = hidden.shape
    block = (rows, width // depth)
    whole = pl.BlockSpec(memory_space=pltpu.VMEM)
    return pl.pallas_call(
        split_kernel,
        out_shape=[jax.ShapeDtypeStruct(block, hidden.dtype)] * depth,
        in_specs=[pl.BlockSpec(memory_space=pltpu.SMEM), whole],
        out_specs=[whole] * depth,
        scratch_shapes=[pltpu.VMEM((depth,) + block, hidden.dtype)],
        compiler_params=pltpu.CompilerParams(vmem_limit_bytes=40 << 20),
    )(level, hidden)


def join_kernel(level_ref, *refs):
    parts, out_ref, held = refs[:-2], refs[-2], refs[-1]
    depth, _, wide = held.shape
    share = wide // 2
    for part, by in zip(parts, distances(depth)):
        held[lax.rem(level_ref[0] + (by + depth), depth)] = part[...]
    for z in range(0, depth, 2):
        for s in range(2):
            pair = [held[z + i, :, s * share : (s + 1) * share] for i in range(2)]
            out_ref[:, (s * depth + z) * share : (s * depth + z + 2) * share] = (
                jnp.concatenate(pair, axis=1)
            )


def join_levels(parts, level):
    depth = len(parts)
    rows, wide = parts[0].shape
    whole = pl.BlockSpec(memory_space=pltpu.VMEM)
    return pl.pallas_call(
        join_kernel,
        out_shape=jax.ShapeDtypeStruct((rows, depth * wide), parts[0].dtype),
        in_specs=[pl.BlockSpec(memory_space=pltpu.SMEM)] + [whole] * depth,
        out_specs=whole,
        scratch_shapes=[pltpu.VMEM((depth, rows, wide), parts[0].dtype)],
        compiler_params=pltpu.CompilerParams(vmem_limit_bytes=40 << 20),
    )(level, *parts)


def halves_of(ref, core, half):
    own = pl.multiple_of(core * half, half)
    return ref[..., pl.ds(own, half)], ref[..., pl.ds(pl.multiple_of(half - own, half), half)]


def join_rows_kernel(place_ref, core_ref, next_ref, own_ref, mate_ref, own_scales, mate_scales, *refs):
    rows_refs, out_ref, passed_ref = refs[:-2], refs[-2], refs[-1]
    for i in range(next_ref.shape[0]):
        passed_ref[i] = next_ref[i]
    half = own_ref.shape[0]
    pairs = [halves_of(ref, core_ref[0], half) for ref in rows_refs]
    own = jnp.concatenate([pair[0][0] for pair in pairs])
    mate = jnp.concatenate([pair[1][0] for pair in pairs])
    total = own_scales[...] * jnp.dot(own, own_ref[...], preferred_element_type=jnp.float32)
    total += mate_scales[...] * jnp.dot(mate, mate_ref[...], preferred_element_type=jnp.float32)
    places, steps, slots, wide = out_ref.shape
    total = total.reshape(steps, places, slots, wide).astype(out_ref.dtype)
    for step in range(steps):
        out_ref[:, step] = total[step]


def join_rows(where, core, then, values, codes, scales, places):
    steps = where.shape[0]
    _, rows, cols = values.shape
    half, wide = codes[0].shape

    def rows_spec(j):
        return pl.BlockSpec((1, rows, cols), lambda i, w, c: (w[j], 0, 0))

    def whole(*shape):
        return pl.BlockSpec(shape, lambda i, w, c: (0,) * len(shape))

    words = pl.BlockSpec(memory_space=pltpu.SMEM)
    shape = (places, steps, rows // places, wide)
    return pl.pallas_call(
        join_rows_kernel,
        out_shape=[pltpu.HBM(shape, jnp.bfloat16), jax.ShapeDtypeStruct(then.shape, then.dtype)],
        grid_spec=pltpu.PrefetchScalarGridSpec(
            num_scalar_prefetch=2,
            grid=(1,),
            in_specs=[words] + [whole(half, wide)] * 2 + [whole(1, wide)] * 2
            + [rows_spec(j) for j in range(steps)],
            out_specs=[whole(*shape), words],
        ),
        compiler_params=pltpu.CompilerParams(vmem_limit_bytes=40 << 20),
    )(where, core, then, *codes, *scales, *[values] * steps)


def weight_kernel(core_ref, values_ref, mate_values_ref, own_ref, mate_ref, out_ref):
    half = out_ref.shape[1]
    own_rows = halves_of(values_ref, core_ref[0], half)[0].reshape(-1, half)
    mate_rows = halves_of(mate_values_ref, core_ref[0], half)[0].reshape(-1, half)
    part = lax.dot_general(
        jnp.concatenate([own_ref[...], mate_ref[...]]),
        jnp.concatenate([own_rows, mate_rows]),
        (((0,), (0,)), ((), ())),
        preferred_element_type=jnp.float32,
    )

    @pl.when(pl.program_id(0) == 0)
    def _():
        out_ref[...] = part

    @pl.when(pl.program_id(0) > 0)
    def _():
        out_ref[...] += part


def weight_sums(core, values, mate_values, own, mate, levels=2):
    depth, rows, cols = values.shape
    wide, half = own.shape[1], cols // 2
    units = pl.BlockSpec((levels * rows, wide), lambda i, c: (i, 0))
    return pl.pallas_call(
        weight_kernel,
        out_shape=pltpu.HBM((wide, half), jnp.float32),
        grid_spec=pltpu.PrefetchScalarGridSpec(
            num_scalar_prefetch=1,
            grid=(depth // levels,),
            in_specs=[
                pl.BlockSpec((levels, rows, cols), lambda i, c: (i, 0, 0)),
                pl.BlockSpec((levels, rows, cols), lambda i, c: (i, 0, 0)),
                units,
                units,
            ],
            out_specs=pl.BlockSpec((wide, half), lambda i, c: (0, 0)),
        ),
        compiler_params=pltpu.CompilerParams(vmem_limit_bytes=40 << 20),
    )(core, values, mate_values, own, mate)


def rows_kernel(counts_ref, rows_ref, out_ref):
    experts, slots, cols = out_ref.shape
    rows = rows_ref.shape[0]
    slot = lax.broadcasted_iota(jnp.int32, (slots, rows), 0)
    row = lax.broadcasted_iota(jnp.int32, (slots, rows), 1)
    hot, start = [], 0
    for e in range(experts):
        count = counts_ref[e]
        hit = jnp.logical_and(row == slot + start, slot < count)
        hot.append(jnp.where(hit, 1.0, 0.0))
        start = start + count
    hot = jnp.concatenate(hot).astype(jnp.bfloat16)
    packed = jnp.dot(hot, rows_ref[...], preferred_element_type=jnp.float32)
    out_ref[...] = packed.reshape(experts, slots, cols).astype(out_ref.dtype)


def pack_rows(counts, cotangent, slots):
    rows, cols = cotangent.shape
    whole = pl.BlockSpec(memory_space=pltpu.VMEM)
    return pl.pallas_call(
        rows_kernel,
        out_shape=jax.ShapeDtypeStruct((counts.shape[0], slots, cols), cotangent.dtype),
        in_specs=[pl.BlockSpec(memory_space=pltpu.SMEM), whole],
        out_specs=whole,
        compiler_params=pltpu.CompilerParams(vmem_limit_bytes=40 << 20),
    )(counts, cotangent)


def unpack_kernel(hot_ref, back_ref, *outs):
    experts, _, slots, wide = back_ref.shape
    for i, out in enumerate(outs):
        packed = back_ref[:, i].astype(jnp.float32).reshape(experts * slots, wide)
        out[...] = lax.dot_general(
            hot_ref[i], packed.astype(jnp.bfloat16), (((0,), (0,)), ((), ())),
            preferred_element_type=jnp.float32,
        ).astype(out.dtype)


def unpack(hot, back):
    steps, _, rows = hot.shape
    whole = pl.BlockSpec(memory_space=pltpu.VMEM)
    return pl.pallas_call(
        unpack_kernel,
        out_shape=[jax.ShapeDtypeStruct((rows, back.shape[-1]), back.dtype)] * steps,
        in_specs=[whole, whole],
        out_specs=[whole] * steps,
        compiler_params=pltpu.CompilerParams(vmem_limit_bytes=40 << 20),
    )(hot, back)


def pack_kernel(level_ref, hot_ref, *refs):
    blocks, out_ref = refs[:-1], refs[-1]
    experts, depth, slots, wide = out_ref.shape
    for i, by in enumerate(distances(depth)):
        packed = jnp.dot(hot_ref[i], blocks[i][...], preferred_element_type=jnp.float32)
        level = lax.rem(level_ref[0] + (by + depth), depth)
        out_ref[:, level] = packed.reshape(experts, slots, wide).astype(out_ref.dtype)


def pack_hidden(hot, blocks, level, experts):
    depth, places, rows = hot.shape
    wide = blocks[0].shape[1]
    whole = pl.BlockSpec(memory_space=pltpu.VMEM)
    return pl.pallas_call(
        pack_kernel,
        out_shape=pltpu.HBM((experts, depth, places // experts, wide), jnp.bfloat16),
        in_specs=[pl.BlockSpec(memory_space=pltpu.SMEM)] + [whole] * (depth + 1),
        out_specs=whole,
        compiler_params=pltpu.CompilerParams(vmem_limit_bytes=40 << 20),
    )(level, hot, *blocks)


def shards(cotangent, hidden, codes, scales, counts):
    rows, cols = cotangent.shape
    half = cols // 2
    share = codes.shape[1]
    places = lax.axis_size(PLACES)
    depth = lax.axis_size("z")
    experts = counts.shape[1]
    slots = 3 * rows // (2 * experts)
    wide = 2 * share
    order = distances(depth)
    place, core = lax.axis_index(PLACES), lax.axis_index("c")
    side, level = lax.axis_index("xl"), lax.axis_index("z")
    core_word = core.astype(jnp.int32).reshape(1)
    level_word = level.astype(jnp.int32).reshape(1)

    def levels_at(steps):
        return (level.astype(jnp.int32) + jnp.array(steps, jnp.int32) + depth) % depth

    line_at = ((place * 2 + core) * 2 + side) * depth
    own_counts = lax.dynamic_slice_in_dim(counts, line_at + level, 1, 0).reshape(experts)
    line_counts = lax.dynamic_slice_in_dim(counts, line_at, depth, 0)
    near_counts = lax.dynamic_slice_in_dim(jnp.concatenate([line_counts] * 2), level, depth, 0)
    near_counts = jnp.stack([near_counts[by % depth] for by in order])
    near_hot = slot_hot(near_counts, slots, rows).reshape(depth, experts * slots, rows)

    other_codes, other_scales = lax.ppermute((codes[0], scales[0]), "xl", SWAP)
    by_level = split_levels(hidden, level_word, depth)

    packed = pack_rows(own_counts, cotangent, slots)
    arrived = lax.all_to_all(packed, PLACES, 0, 0).reshape(places * slots, cols)

    line_hidden = {}
    for block, by in zip(by_level, order):
        line_hidden[-by if by < depth // 2 else by] = along_z(block, by) if by else block
    arrived, line_hidden[-1], line_hidden[1] = lax.optimization_barrier(
        (arrived, line_hidden[-1], line_hidden[1])
    )
    values = lax.all_gather(arrived, "z", axis=0, tiled=True)
    values = values.reshape(depth, places * slots, cols)

    first = side == 0
    both_codes = jnp.where(first, jnp.stack([codes[0], other_codes]),
                           jnp.stack([other_codes, codes[0]])).reshape(wide, half).T
    both_scales = jnp.where(first, jnp.stack([scales[0], other_scales]),
                            jnp.stack([other_scales, scales[0]])).reshape(1, wide)
    mate_scales, mate_codes = lax.ppermute((both_scales, both_codes), "c", SWAP)
    both_codes, both_scales, mate_codes, mate_scales, *line_hidden = lax.optimization_barrier(
        [both_codes, both_scales, mate_codes, mate_scales] + [line_hidden[by] for by in order]
    )

    hidden_slots = pack_hidden(near_hot, line_hidden, level_word, experts)
    own_hidden = lax.all_to_all(hidden_slots, PLACES, 0, 0)
    own_hidden = own_hidden.transpose(1, 0, 2, 3).reshape(depth * places * slots, wide)
    mate_hidden = lax.ppermute(own_hidden, "c", SWAP)
    values = after(values, own_hidden)
    gathered = values
    values = pltpu.with_memory_space_constraint(values, pltpu.HBM)

    def join(where, then):
        return join_rows(
            where, core_word, then, values, (both_codes, mate_codes), (both_scales, mate_scales), places
        )

    came = {}

    def send_home(steps, back):
        for by, block in zip(steps, back):
            came[-by if by < depth // 2 else by] = along_z(block, by) if by else block

    cut = 3
    far_at, close_at = levels_at(order[:cut]), levels_at(order[cut:])
    far_joined, close_at = join(far_at, close_at)
    close_joined, _ = join(close_at, far_at)
    mate_values = lax.ppermute(gathered, "c", SWAP)
    far_raw = after(lax.all_to_all(far_joined, PLACES, 0, 0), close_joined)
    far_back = unpack(near_hot[:cut], far_raw)
    send_home(order[:cut], far_back)
    own_hidden, mate_hidden = after((own_hidden, mate_hidden), *far_back)
    sums = weight_sums(core_word, values, mate_values, own_hidden, mate_hidden)
    close_raw = after(lax.all_to_all(close_joined, PLACES, 0, 0), *came.values(), sums)
    send_home(order[cut:], unpack(near_hot[cut:], close_raw))

    sums = sums.reshape(2, share, half)
    gone = lax.dynamic_index_in_dim(sums, 1 - side, 0, keepdims=False)
    kept = lax.dynamic_index_in_dim(sums, side, 0, keepdims=False)
    largest = jnp.maximum(jnp.max(jnp.abs(gone)), 1e-30).reshape(1)
    gone = (gone * (1 / largest)).astype(jnp.float16)
    largest = lax.ppermute(largest, "xl", SWAP)
    gone, kept, largest, _ = lax.optimization_barrier((gone, kept, largest, close_raw))
    gone = lax.ppermute(gone, "xl", SWAP)
    weight_grad = kept + gone.astype(jnp.float32) * largest
    d_hidden = join_levels([came[by] for by in order], after(level_word, weight_grad))
    return d_hidden, weight_grad[None]


def solution(mesh):
    lanes, lines = mesh.devices.shape
    fine = Mesh(mesh.devices.reshape(2, lanes // 4, 2, 2, lines // 2), ("xh", "y", "c", "xl", "z"))
    expert, dp = ("xh", "y", "c"), ("xl", "z")
    in_specs = (P(expert + dp, None), P(expert + dp, None), P(expert, dp, None), P(expert, dp), P())
    out_specs = (P(expert + dp, None), P(expert, dp, None))
    return jax.shard_map(shards, mesh=fine, in_specs=in_specs, out_specs=out_specs, check_vma=False)
```

```python
import jax
import jax.numpy as jnp
from jax import lax
from jax.experimental import pallas as pl
from jax.experimental.pallas import tpu as pltpu
from jax.sharding import Mesh, PartitionSpec as P

PLACES = ("xh", "y")
SWAP = [(0, 1), (1, 0)]


def slot_hot(row_counts, slots, rows):
    starts = jnp.cumsum(row_counts, axis=-1) - row_counts
    slot = jnp.arange(slots, dtype=jnp.int32)
    source = jnp.where(slot < row_counts[..., None], starts[..., None] + slot, -1)
    return (source[..., None] == jnp.arange(rows, dtype=jnp.int32)).astype(jnp.bfloat16)


def distances(depth):
    order = [depth // 2]
    for k in range(depth // 2 - 1, 0, -1):
        order += [k, -k]
    return order + [0]


def after(value, *others):
    return lax.optimization_barrier((value,) + others)[0]


def along_z(value, by):
    depth = lax.axis_size("z")
    return lax.ppermute(value, "z", [(i, (i + by) % depth) for i in range(depth)])


def split_kernel(level_ref, hidden_ref, *refs):
    outs, held = refs[:-1], refs[-1]
    depth, _, wide = held.shape
    share = wide // 2
    for z in range(depth):
        low = hidden_ref[:, z * share : (z + 1) * share]
        high = hidden_ref[:, (depth + z) * share : (depth + z + 1) * share]
        held[z] = jnp.concatenate([low, high], axis=1)
    for out, by in zip(outs, distances(depth)):
        out[...] = held[lax.rem(level_ref[0] + (by + depth), depth)]


def split_levels(hidden, level, depth):
    rows, width = hidden.shape
    block = (rows, width // depth)
    whole = pl.BlockSpec(memory_space=pltpu.VMEM)
    return pl.pallas_call(
        split_kernel,
        out_shape=[jax.ShapeDtypeStruct(block, hidden.dtype)] * depth,
        in_specs=[pl.BlockSpec(memory_space=pltpu.SMEM), whole],
        out_specs=[whole] * depth,
        scratch_shapes=[pltpu.VMEM((depth,) + block, hidden.dtype)],
        compiler_params=pltpu.CompilerParams(vmem_limit_bytes=40 << 20),
    )(level, hidden)


def join_kernel(level_ref, *refs):
    parts, out_ref, held = refs[:-2], refs[-2], refs[-1]
    depth, _, wide = held.shape
    share = wide // 2
    for part, by in zip(parts, distances(depth)):
        held[lax.rem(level_ref[0] + (by + depth), depth)] = part[...]
    for z in range(0, depth, 2):
        for s in range(2):
            pair = [held[z + i, :, s * share : (s + 1) * share] for i in range(2)]
            out_ref[:, (s * depth + z) * share : (s * depth + z + 2) * share] = (
                jnp.concatenate(pair, axis=1)
            )


def join_levels(parts, level):
    depth = len(parts)
    rows, wide = parts[0].shape
    whole = pl.BlockSpec(memory_space=pltpu.VMEM)
    return pl.pallas_call(
        join_kernel,
        out_shape=jax.ShapeDtypeStruct((rows, depth * wide), parts[0].dtype),
        in_specs=[pl.BlockSpec(memory_space=pltpu.SMEM)] + [whole] * depth,
        out_specs=whole,
        scratch_shapes=[pltpu.VMEM((depth, rows, wide), parts[0].dtype)],
        compiler_params=pltpu.CompilerParams(vmem_limit_bytes=40 << 20),
    )(level, *parts)


def halves_of(ref, core, half):
    own = pl.multiple_of(core * half, half)
    return ref[..., pl.ds(own, half)], ref[..., pl.ds(pl.multiple_of(half - own, half), half)]


def join_rows_kernel(place_ref, core_ref, next_ref, own_ref, mate_ref, own_scales, mate_scales, *refs):
    rows_refs, out_ref, passed_ref = refs[:-2], refs[-2], refs[-1]
    for i in range(next_ref.shape[0]):
        passed_ref[i] = next_ref[i]
    half = own_ref.shape[0]
    pairs = [halves_of(ref, core_ref[0], half) for ref in rows_refs]
    own = jnp.concatenate([pair[0][0] for pair in pairs])
    mate = jnp.concatenate([pair[1][0] for pair in pairs])
    total = own_scales[...] * jnp.dot(own, own_ref[...], preferred_element_type=jnp.float32)
    total += mate_scales[...] * jnp.dot(mate, mate_ref[...], preferred_element_type=jnp.float32)
    places, steps, slots, wide = out_ref.shape
    total = total.reshape(steps, places, slots, wide).astype(out_ref.dtype)
    for step in range(steps):
        out_ref[:, step] = total[step]


def join_rows(where, core, then, values, codes, scales, places):
    steps = where.shape[0]
    _, rows, cols = values.shape
    half, wide = codes[0].shape

    def rows_spec(j):
        return pl.BlockSpec((1, rows, cols), lambda i, w, c: (w[j], 0, 0))

    def whole(*shape):
        return pl.BlockSpec(shape, lambda i, w, c: (0,) * len(shape))

    words = pl.BlockSpec(memory_space=pltpu.SMEM)
    shape = (places, steps, rows // places, wide)
    return pl.pallas_call(
        join_rows_kernel,
        out_shape=[pltpu.HBM(shape, jnp.bfloat16), jax.ShapeDtypeStruct(then.shape, then.dtype)],
        grid_spec=pltpu.PrefetchScalarGridSpec(
            num_scalar_prefetch=2,
            grid=(1,),
            in_specs=[words] + [whole(half, wide)] * 2 + [whole(1, wide)] * 2
            + [rows_spec(j) for j in range(steps)],
            out_specs=[whole(*shape), words],
        ),
        compiler_params=pltpu.CompilerParams(vmem_limit_bytes=40 << 20),
    )(where, core, then, *codes, *scales, *[values] * steps)


def weight_kernel(core_ref, values_ref, mate_values_ref, own_ref, mate_ref, out_ref):
    half = out_ref.shape[1]
    own_rows = halves_of(values_ref, core_ref[0], half)[0].reshape(-1, half)
    mate_rows = halves_of(mate_values_ref, core_ref[0], half)[0].reshape(-1, half)
    part = lax.dot_general(
        jnp.concatenate([own_ref[...], mate_ref[...]]),
        jnp.concatenate([own_rows, mate_rows]),
        (((0,), (0,)), ((), ())),
        preferred_element_type=jnp.float32,
    )

    @pl.when(pl.program_id(0) == 0)
    def _():
        out_ref[...] = part

    @pl.when(pl.program_id(0) > 0)
    def _():
        out_ref[...] += part


def weight_sums(core, values, mate_values, own, mate, levels=2):
    depth, rows, cols = values.shape
    wide, half = own.shape[1], cols // 2
    units = pl.BlockSpec((levels * rows, wide), lambda i, c: (i, 0))
    return pl.pallas_call(
        weight_kernel,
        out_shape=pltpu.HBM((wide, half), jnp.float32),
        grid_spec=pltpu.PrefetchScalarGridSpec(
            num_scalar_prefetch=1,
            grid=(depth // levels,),
            in_specs=[
                pl.BlockSpec((levels, rows, cols), lambda i, c: (i, 0, 0)),
                pl.BlockSpec((levels, rows, cols), lambda i, c: (i, 0, 0)),
                units,
                units,
            ],
            out_specs=pl.BlockSpec((wide, half), lambda i, c: (0, 0)),
        ),
        compiler_params=pltpu.CompilerParams(vmem_limit_bytes=40 << 20),
    )(core, values, mate_values, own, mate)


def rows_kernel(counts_ref, rows_ref, out_ref):
    experts, slots, cols = out_ref.shape
    rows = rows_ref.shape[0]
    slot = lax.broadcasted_iota(jnp.int32, (slots, rows), 0)
    row = lax.broadcasted_iota(jnp.int32, (slots, rows), 1)
    hot, start = [], 0
    for e in range(experts):
        count = counts_ref[e]
        hit = jnp.logical_and(row == slot + start, slot < count)
        hot.append(jnp.where(hit, 1.0, 0.0))
        start = start + count
    hot = jnp.concatenate(hot).astype(jnp.bfloat16)
    packed = jnp.dot(hot, rows_ref[...], preferred_element_type=jnp.float32)
    out_ref[...] = packed.reshape(experts, slots, cols).astype(out_ref.dtype)


def pack_rows(counts, cotangent, slots):
    rows, cols = cotangent.shape
    whole = pl.BlockSpec(memory_space=pltpu.VMEM)
    return pl.pallas_call(
        rows_kernel,
        out_shape=jax.ShapeDtypeStruct((counts.shape[0], slots, cols), cotangent.dtype),
        in_specs=[pl.BlockSpec(memory_space=pltpu.SMEM), whole],
        out_specs=whole,
        compiler_params=pltpu.CompilerParams(vmem_limit_bytes=40 << 20),
    )(counts, cotangent)


def unpack_kernel(hot_ref, back_ref, *outs):
    experts, _, slots, wide = back_ref.shape
    for i, out in enumerate(outs):
        packed = back_ref[:, i].astype(jnp.float32).reshape(experts * slots, wide)
        out[...] = lax.dot_general(
            hot_ref[i], packed.astype(jnp.bfloat16), (((0,), (0,)), ((), ())),
            preferred_element_type=jnp.float32,
        ).astype(out.dtype)


def unpack(hot, back):
    steps, _, rows = hot.shape
    whole = pl.BlockSpec(memory_space=pltpu.VMEM)
    return pl.pallas_call(
        unpack_kernel,
        out_shape=[jax.ShapeDtypeStruct((rows, back.shape[-1]), back.dtype)] * steps,
        in_specs=[whole, whole],
        out_specs=[whole] * steps,
        compiler_params=pltpu.CompilerParams(vmem_limit_bytes=40 << 20),
    )(hot, back)


def pack_kernel(level_ref, hot_ref, *refs):
    blocks, out_ref = refs[:-1], refs[-1]
    experts, depth, slots, wide = out_ref.shape
    for i, by in enumerate(distances(depth)):
        packed = jnp.dot(hot_ref[i], blocks[i][...], preferred_element_type=jnp.float32)
        level = lax.rem(level_ref[0] + (by + depth), depth)
        out_ref[:, level] = packed.reshape(experts, slots, wide).astype(out_ref.dtype)


def pack_hidden(hot, blocks, level, experts):
    depth, places, rows = hot.shape
    wide = blocks[0].shape[1]
    whole = pl.BlockSpec(memory_space=pltpu.VMEM)
    return pl.pallas_call(
        pack_kernel,
        out_shape=pltpu.HBM((experts, depth, places // experts, wide), jnp.bfloat16),
        in_specs=[pl.BlockSpec(memory_space=pltpu.SMEM)] + [whole] * (depth + 1),
        out_specs=whole,
        compiler_params=pltpu.CompilerParams(vmem_limit_bytes=40 << 20),
    )(level, hot, *blocks)


def shards(cotangent, hidden, codes, scales, counts):
    rows, cols = cotangent.shape
    half = cols // 2
    share = codes.shape[1]
    places = lax.axis_size(PLACES)
    depth = lax.axis_size("z")
    experts = counts.shape[1]
    slots = 3 * rows // (2 * experts)
    wide = 2 * share
    order = distances(depth)
    place, core = lax.axis_index(PLACES), lax.axis_index("c")
    side, level = lax.axis_index("xl"), lax.axis_index("z")
    core_word = core.astype(jnp.int32).reshape(1)
    level_word = level.astype(jnp.int32).reshape(1)

    def levels_at(steps):
        return (level.astype(jnp.int32) + jnp.array(steps, jnp.int32) + depth) % depth

    line_at = ((place * 2 + core) * 2 + side) * depth
    own_counts = lax.dynamic_slice_in_dim(counts, line_at + level, 1, 0).reshape(experts)
    line_counts = lax.dynamic_slice_in_dim(counts, line_at, depth, 0)
    near_counts = lax.dynamic_slice_in_dim(jnp.concatenate([line_counts] * 2), level, depth, 0)
    near_counts = jnp.stack([near_counts[by % depth] for by in order])
    near_hot = slot_hot(near_counts, slots, rows).reshape(depth, experts * slots, rows)

    other_codes, other_scales = lax.ppermute((codes[0], scales[0]), "xl", SWAP)
    by_level = split_levels(hidden, level_word, depth)

    packed = pack_rows(own_counts, cotangent, slots)
    arrived = lax.all_to_all(packed, PLACES, 0, 0).reshape(places * slots, cols)

    line_hidden = {}
    for block, by in zip(by_level, order):
        line_hidden[-by if by < depth // 2 else by] = along_z(block, by) if by else block
    arrived, line_hidden[-1], line_hidden[1] = lax.optimization_barrier(
        (arrived, line_hidden[-1], line_hidden[1])
    )
    values = lax.all_gather(arrived, "z", axis=0, tiled=True)
    values = values.reshape(depth, places * slots, cols)

    other_codes, other_scales, *line_hidden = lax.optimization_barrier(
        [other_codes, other_scales] + [line_hidden[by] for by in order]
    )

    hidden_slots = pack_hidden(near_hot, line_hidden, level_word, experts)
    other_codes, other_scales = after((other_codes, other_scales), hidden_slots)
    first = side == 0
    both_codes = jnp.where(first, jnp.stack([codes[0], other_codes]),
                           jnp.stack([other_codes, codes[0]])).reshape(wide, half).T
    both_scales = jnp.where(first, jnp.stack([scales[0], other_scales]),
                            jnp.stack([other_scales, scales[0]])).reshape(1, wide)
    mate_scales, mate_codes = lax.ppermute((both_scales, both_codes), "c", SWAP)

    own_hidden = lax.all_to_all(hidden_slots, PLACES, 0, 0)
    own_hidden = own_hidden.transpose(1, 0, 2, 3).reshape(depth * places * slots, wide)
    mate_hidden = lax.ppermute(own_hidden, "c", SWAP)
    values, mate_codes, mate_scales = lax.optimization_barrier((values, mate_codes, mate_scales))
    values = after(values, own_hidden)
    gathered = values
    values = pltpu.with_memory_space_constraint(values, pltpu.HBM)

    def join(where, then):
        return join_rows(
            where, core_word, then, values, (both_codes, mate_codes), (both_scales, mate_scales), places
        )

    came = {}

    def send_home(steps, back):
        for by, block in zip(steps, back):
            came[-by if by < depth // 2 else by] = along_z(block, by) if by else block

    cut = 3
    far_at, close_at = levels_at(order[:cut]), levels_at(order[cut:])
    far_joined, close_at = join(far_at, close_at)
    close_joined, _ = join(close_at, far_at)
    mate_values = lax.ppermute(gathered, "c", SWAP)
    far_raw = after(lax.all_to_all(far_joined, PLACES, 0, 0), close_joined)
    far_back = unpack(near_hot[:cut], far_raw)
    send_home(order[:cut], far_back)
    own_hidden, mate_hidden = after((own_hidden, mate_hidden), *far_back)
    sums = weight_sums(core_word, values, mate_values, own_hidden, mate_hidden)
    close_raw = after(lax.all_to_all(close_joined, PLACES, 0, 0), *came.values(), sums)
    send_home(order[cut:], unpack(near_hot[cut:], close_raw))

    sums = sums.reshape(2, share, half)
    gone = lax.dynamic_index_in_dim(sums, 1 - side, 0, keepdims=False)
    kept = lax.dynamic_index_in_dim(sums, side, 0, keepdims=False)
    largest = jnp.maximum(jnp.max(jnp.abs(gone)), 1e-30).reshape(1)
    gone = (gone * (1 / largest)).astype(jnp.float16)
    largest = lax.ppermute(largest, "xl", SWAP)
    gone, kept, largest, _ = lax.optimization_barrier((gone, kept, largest, close_raw))
    gone = lax.ppermute(gone, "xl", SWAP)
    weight_grad = kept + gone.astype(jnp.float32) * largest
    d_hidden = join_levels([came[by] for by in order], after(level_word, weight_grad))
    return d_hidden, weight_grad[None]


def solution(mesh):
    lanes, lines = mesh.devices.shape
    fine = Mesh(mesh.devices.reshape(2, lanes // 4, 2, 2, lines // 2), ("xh", "y", "c", "xl", "z"))
    expert, dp = ("xh", "y", "c"), ("xl", "z")
    in_specs = (P(expert + dp, None), P(expert + dp, None), P(expert, dp, None), P(expert, dp), P())
    out_specs = (P(expert + dp, None), P(expert, dp, None))
    return jax.shard_map(shards, mesh=fine, in_specs=in_specs, out_specs=out_specs, check_vma=False)
```

```python
import jax
import jax.numpy as jnp
from jax import lax
from jax.experimental import pallas as pl
from jax.experimental.pallas import tpu as pltpu
from jax.sharding import Mesh, PartitionSpec as P

PLACES = ("xh", "y")
SWAP = [(0, 1), (1, 0)]


def slot_hot(row_counts, slots, rows):
    starts = jnp.cumsum(row_counts, axis=-1) - row_counts
    slot = jnp.arange(slots, dtype=jnp.int32)
    source = jnp.where(slot < row_counts[..., None], starts[..., None] + slot, -1)
    return (source[..., None] == jnp.arange(rows, dtype=jnp.int32)).astype(jnp.bfloat16)


def distances(depth):
    order = [depth // 2]
    for k in range(depth // 2 - 1, 0, -1):
        order += [k, -k]
    return order + [0]


def after(value, *others):
    return lax.optimization_barrier((value,) + others)[0]


def along_z(value, by):
    depth = lax.axis_size("z")
    return lax.ppermute(value, "z", [(i, (i + by) % depth) for i in range(depth)])


def split_kernel(level_ref, hidden_ref, *refs):
    outs, held = refs[:-1], refs[-1]
    depth, _, wide = held.shape
    share = wide // 2
    for z in range(depth):
        low = hidden_ref[:, z * share : (z + 1) * share]
        high = hidden_ref[:, (depth + z) * share : (depth + z + 1) * share]
        held[z] = jnp.concatenate([low, high], axis=1)
    for out, by in zip(outs, distances(depth)):
        out[...] = held[lax.rem(level_ref[0] + (by + depth), depth)]


def split_levels(hidden, level, depth):
    rows, width = hidden.shape
    block = (rows, width // depth)
    whole = pl.BlockSpec(memory_space=pltpu.VMEM)
    return pl.pallas_call(
        split_kernel,
        out_shape=[jax.ShapeDtypeStruct(block, hidden.dtype)] * depth,
        in_specs=[pl.BlockSpec(memory_space=pltpu.SMEM), whole],
        out_specs=[whole] * depth,
        scratch_shapes=[pltpu.VMEM((depth,) + block, hidden.dtype)],
        compiler_params=pltpu.CompilerParams(vmem_limit_bytes=40 << 20),
    )(level, hidden)


def join_kernel(level_ref, *refs):
    parts, out_ref, held = refs[:-2], refs[-2], refs[-1]
    depth, _, wide = held.shape
    share = wide // 2
    for part, by in zip(parts, distances(depth)):
        held[lax.rem(level_ref[0] + (by + depth), depth)] = part[...]
    for z in range(0, depth, 2):
        for s in range(2):
            pair = [held[z + i, :, s * share : (s + 1) * share] for i in range(2)]
            out_ref[:, (s * depth + z) * share : (s * depth + z + 2) * share] = (
                jnp.concatenate(pair, axis=1)
            )


def join_levels(parts, level):
    depth = len(parts)
    rows, wide = parts[0].shape
    whole = pl.BlockSpec(memory_space=pltpu.VMEM)
    return pl.pallas_call(
        join_kernel,
        out_shape=jax.ShapeDtypeStruct((rows, depth * wide), parts[0].dtype),
        in_specs=[pl.BlockSpec(memory_space=pltpu.SMEM)] + [whole] * depth,
        out_specs=whole,
        scratch_shapes=[pltpu.VMEM((depth, rows, wide), parts[0].dtype)],
        compiler_params=pltpu.CompilerParams(vmem_limit_bytes=40 << 20),
    )(level, *parts)


def halves_of(ref, core, half):
    own = pl.multiple_of(core * half, half)
    return ref[..., pl.ds(own, half)], ref[..., pl.ds(pl.multiple_of(half - own, half), half)]


def join_rows_kernel(place_ref, core_ref, next_ref, own_ref, mate_ref, own_scales, mate_scales, *refs):
    rows_refs, out_ref, passed_ref, held = refs[:-3], refs[-3], refs[-2], refs[-1]
    for i in range(next_ref.shape[0]):
        passed_ref[i] = next_ref[i]
    values = jnp.concatenate([ref[0] for ref in rows_refs])

    @pl.when(pl.program_id(0) == 0)
    def _():
        held[...] = own_scales[...] * jnp.dot(
            values, own_ref[...], preferred_element_type=jnp.float32
        )

    @pl.when(pl.program_id(0) == 1)
    def _():
        total = held[...] + mate_scales[...] * jnp.dot(
            values, mate_ref[...], preferred_element_type=jnp.float32
        )
        places, steps, slots, wide = out_ref.shape
        total = total.reshape(steps, places, slots, wide).astype(out_ref.dtype)
        for step in range(steps):
            out_ref[:, step] = total[step]


def join_rows(where, core, then, values, codes, scales, places):
    steps = where.shape[0]
    _, rows, cols = values.shape
    half, wide = codes[0].shape

    def rows_spec(j):
        return pl.BlockSpec((1, rows, half), lambda i, w, c: (w[j], 0, c[0] ^ i))

    def whole(*shape):
        return pl.BlockSpec(shape, lambda i, w, c: (0,) * len(shape))

    words = pl.BlockSpec(memory_space=pltpu.SMEM)
    shape = (places, steps, rows // places, wide)
    return pl.pallas_call(
        join_rows_kernel,
        out_shape=[pltpu.HBM(shape, jnp.bfloat16), jax.ShapeDtypeStruct(then.shape, then.dtype)],
        grid_spec=pltpu.PrefetchScalarGridSpec(
            num_scalar_prefetch=2,
            grid=(2,),
            in_specs=[words] + [whole(half, wide)] * 2 + [whole(1, wide)] * 2
            + [rows_spec(j) for j in range(steps)],
            out_specs=[whole(*shape), words],
            scratch_shapes=[pltpu.VMEM((steps * rows, wide), jnp.float32)],
        ),
        compiler_params=pltpu.CompilerParams(vmem_limit_bytes=40 << 20),
    )(where, core, then, *codes, *scales, *[values] * steps)


def weight_kernel(core_ref, values_ref, mate_values_ref, own_ref, mate_ref, out_ref):
    half = out_ref.shape[1]
    own_rows = halves_of(values_ref, core_ref[0], half)[0].reshape(-1, half)
    mate_rows = halves_of(mate_values_ref, core_ref[0], half)[0].reshape(-1, half)
    part = lax.dot_general(
        jnp.concatenate([own_ref[...], mate_ref[...]]),
        jnp.concatenate([own_rows, mate_rows]),
        (((0,), (0,)), ((), ())),
        preferred_element_type=jnp.float32,
    )

    @pl.when(pl.program_id(0) == 0)
    def _():
        out_ref[...] = part

    @pl.when(pl.program_id(0) > 0)
    def _():
        out_ref[...] += part


def weight_sums(core, values, mate_values, own, mate, levels=2):
    depth, rows, cols = values.shape
    wide, half = own.shape[1], cols // 2
    units = pl.BlockSpec((levels * rows, wide), lambda i, c: (i, 0))
    return pl.pallas_call(
        weight_kernel,
        out_shape=pltpu.HBM((wide, half), jnp.float32),
        grid_spec=pltpu.PrefetchScalarGridSpec(
            num_scalar_prefetch=1,
            grid=(depth // levels,),
            in_specs=[
                pl.BlockSpec((levels, rows, cols), lambda i, c: (i, 0, 0)),
                pl.BlockSpec((levels, rows, cols), lambda i, c: (i, 0, 0)),
                units,
                units,
            ],
            out_specs=pl.BlockSpec((wide, half), lambda i, c: (0, 0)),
        ),
        compiler_params=pltpu.CompilerParams(vmem_limit_bytes=40 << 20),
    )(core, values, mate_values, own, mate)


def rows_kernel(counts_ref, rows_ref, out_ref):
    experts, slots, cols = out_ref.shape
    rows = rows_ref.shape[0]
    slot = lax.broadcasted_iota(jnp.int32, (slots, rows), 0)
    row = lax.broadcasted_iota(jnp.int32, (slots, rows), 1)
    hot, start = [], 0
    for e in range(experts):
        count = counts_ref[e]
        hit = jnp.logical_and(row == slot + start, slot < count)
        hot.append(jnp.where(hit, 1.0, 0.0))
        start = start + count
    hot = jnp.concatenate(hot).astype(jnp.bfloat16)
    packed = jnp.dot(hot, rows_ref[...], preferred_element_type=jnp.float32)
    out_ref[...] = packed.reshape(experts, slots, cols).astype(out_ref.dtype)


def pack_rows(counts, cotangent, slots):
    rows, cols = cotangent.shape
    whole = pl.BlockSpec(memory_space=pltpu.VMEM)
    return pl.pallas_call(
        rows_kernel,
        out_shape=jax.ShapeDtypeStruct((counts.shape[0], slots, cols), cotangent.dtype),
        in_specs=[pl.BlockSpec(memory_space=pltpu.SMEM), whole],
        out_specs=whole,
        compiler_params=pltpu.CompilerParams(vmem_limit_bytes=40 << 20),
    )(counts, cotangent)


def unpack_kernel(hot_ref, back_ref, *outs):
    experts, _, slots, wide = back_ref.shape
    for i, out in enumerate(outs):
        packed = back_ref[:, i].astype(jnp.float32).reshape(experts * slots, wide)
        out[...] = lax.dot_general(
            hot_ref[i], packed.astype(jnp.bfloat16), (((0,), (0,)), ((), ())),
            preferred_element_type=jnp.float32,
        ).astype(out.dtype)


def unpack(hot, back):
    steps, _, rows = hot.shape
    whole = pl.BlockSpec(memory_space=pltpu.VMEM)
    return pl.pallas_call(
        unpack_kernel,
        out_shape=[jax.ShapeDtypeStruct((rows, back.shape[-1]), back.dtype)] * steps,
        in_specs=[whole, whole],
        out_specs=[whole] * steps,
        compiler_params=pltpu.CompilerParams(vmem_limit_bytes=40 << 20),
    )(hot, back)


def pack_kernel(level_ref, hot_ref, *refs):
    blocks, out_ref = refs[:-1], refs[-1]
    experts, depth, slots, wide = out_ref.shape
    for i, by in enumerate(distances(depth)):
        packed = jnp.dot(hot_ref[i], blocks[i][...], preferred_element_type=jnp.float32)
        level = lax.rem(level_ref[0] + (by + depth), depth)
        out_ref[:, level] = packed.reshape(experts, slots, wide).astype(out_ref.dtype)


def pack_hidden(hot, blocks, level, experts):
    depth, places, rows = hot.shape
    wide = blocks[0].shape[1]
    whole = pl.BlockSpec(memory_space=pltpu.VMEM)
    return pl.pallas_call(
        pack_kernel,
        out_shape=pltpu.HBM((experts, depth, places // experts, wide), jnp.bfloat16),
        in_specs=[pl.BlockSpec(memory_space=pltpu.SMEM)] + [whole] * (depth + 1),
        out_specs=whole,
        compiler_params=pltpu.CompilerParams(vmem_limit_bytes=40 << 20),
    )(level, hot, *blocks)


def shards(cotangent, hidden, codes, scales, counts):
    rows, cols = cotangent.shape
    half = cols // 2
    share = codes.shape[1]
    places = lax.axis_size(PLACES)
    depth = lax.axis_size("z")
    experts = counts.shape[1]
    slots = 3 * rows // (2 * experts)
    wide = 2 * share
    order = distances(depth)
    place, core = lax.axis_index(PLACES), lax.axis_index("c")
    side, level = lax.axis_index("xl"), lax.axis_index("z")
    core_word = core.astype(jnp.int32).reshape(1)
    level_word = level.astype(jnp.int32).reshape(1)

    def levels_at(steps):
        return (level.astype(jnp.int32) + jnp.array(steps, jnp.int32) + depth) % depth

    line_at = ((place * 2 + core) * 2 + side) * depth
    own_counts = lax.dynamic_slice_in_dim(counts, line_at + level, 1, 0).reshape(experts)
    line_counts = lax.dynamic_slice_in_dim(counts, line_at, depth, 0)
    near_counts = lax.dynamic_slice_in_dim(jnp.concatenate([line_counts] * 2), level, depth, 0)
    near_counts = jnp.stack([near_counts[by % depth] for by in order])
    near_hot = slot_hot(near_counts, slots, rows).reshape(depth, experts * slots, rows)

    other_codes, other_scales = lax.ppermute((codes[0], scales[0]), "xl", SWAP)
    by_level = split_levels(hidden, level_word, depth)

    packed = pack_rows(own_counts, cotangent, slots)
    arrived = lax.all_to_all(packed, PLACES, 0, 0).reshape(places * slots, cols)

    line_hidden = {}
    for block, by in zip(by_level, order):
        line_hidden[-by if by < depth // 2 else by] = along_z(block, by) if by else block
    arrived, line_hidden[-1], line_hidden[1] = lax.optimization_barrier(
        (arrived, line_hidden[-1], line_hidden[1])
    )
    values = lax.all_gather(arrived, "z", axis=0, tiled=True)
    values = values.reshape(depth, places * slots, cols)

    other_codes, other_scales, *line_hidden = lax.optimization_barrier(
        [other_codes, other_scales] + [line_hidden[by] for by in order]
    )

    hidden_slots = pack_hidden(near_hot, line_hidden, level_word, experts)
    other_codes, other_scales = after((other_codes, other_scales), hidden_slots)
    first = side == 0
    both_codes = jnp.where(first, jnp.stack([codes[0], other_codes]),
                           jnp.stack([other_codes, codes[0]])).reshape(wide, half).T
    both_scales = jnp.where(first, jnp.stack([scales[0], other_scales]),
                            jnp.stack([other_scales, scales[0]])).reshape(1, wide)
    mate_scales, mate_codes = lax.ppermute((both_scales, both_codes), "c", SWAP)

    own_hidden = lax.all_to_all(hidden_slots, PLACES, 0, 0)
    own_hidden = own_hidden.transpose(1, 0, 2, 3).reshape(depth * places * slots, wide)
    mate_hidden = lax.ppermute(own_hidden, "c", SWAP)
    values, mate_codes, mate_scales = lax.optimization_barrier((values, mate_codes, mate_scales))
    values = after(values, own_hidden)
    gathered = values
    values = pltpu.with_memory_space_constraint(values, pltpu.HBM)

    def join(where, then):
        return join_rows(
            where, core_word, then, values, (both_codes, mate_codes), (both_scales, mate_scales), places
        )

    came = {}

    def send_home(steps, back):
        for by, block in zip(steps, back):
            came[-by if by < depth // 2 else by] = along_z(block, by) if by else block

    cut = 3
    far_at, close_at = levels_at(order[:cut]), levels_at(order[cut:])
    far_joined, close_at = join(far_at, close_at)
    close_joined, _ = join(close_at, far_at)
    mate_values = lax.ppermute(gathered, "c", SWAP)
    far_raw = after(lax.all_to_all(far_joined, PLACES, 0, 0), close_joined)
    far_raw = pltpu.with_memory_space_constraint(far_raw, pltpu.HBM)
    far_back = unpack(near_hot[:cut], far_raw)
    send_home(order[:cut], far_back)
    own_hidden, mate_hidden = after((own_hidden, mate_hidden), *far_back)
    sums = weight_sums(core_word, values, mate_values, own_hidden, mate_hidden)
    close_raw = after(lax.all_to_all(close_joined, PLACES, 0, 0), *came.values(), sums)
    send_home(order[cut:], unpack(near_hot[cut:], close_raw))

    sums = sums.reshape(2, share, half)
    gone = lax.dynamic_index_in_dim(sums, 1 - side, 0, keepdims=False)
    kept = lax.dynamic_index_in_dim(sums, side, 0, keepdims=False)
    largest = jnp.maximum(jnp.max(jnp.abs(gone)), 1e-30).reshape(1)
    gone = (gone * (1 / largest)).astype(jnp.float16)
    largest = lax.ppermute(largest, "xl", SWAP)
    gone, kept, largest, _ = lax.optimization_barrier((gone, kept, largest, close_raw))
    gone = lax.ppermute(gone, "xl", SWAP)
    weight_grad = kept + gone.astype(jnp.float32) * largest
    d_hidden = join_levels([came[by] for by in order], after(level_word, weight_grad))
    return d_hidden, weight_grad[None]


def solution(mesh):
    lanes, lines = mesh.devices.shape
    fine = Mesh(mesh.devices.reshape(2, lanes // 4, 2, 2, lines // 2), ("xh", "y", "c", "xl", "z"))
    expert, dp = ("xh", "y", "c"), ("xl", "z")
    in_specs = (P(expert + dp, None), P(expert + dp, None), P(expert, dp, None), P(expert, dp), P())
    out_specs = (P(expert + dp, None), P(expert, dp, None))
    return jax.shard_map(shards, mesh=fine, in_specs=in_specs, out_specs=out_specs, check_vma=False)
```

```python
import jax
import jax.numpy as jnp
from jax import lax
from jax.experimental import pallas as pl
from jax.experimental.pallas import tpu as pltpu
from jax.sharding import Mesh, PartitionSpec as P

PLACES = ("xh", "y")
SWAP = [(0, 1), (1, 0)]


def slot_hot(row_counts, slots, rows):
    starts = jnp.cumsum(row_counts, axis=-1) - row_counts
    slot = jnp.arange(slots, dtype=jnp.int32)
    source = jnp.where(slot < row_counts[..., None], starts[..., None] + slot, -1)
    return (source[..., None] == jnp.arange(rows, dtype=jnp.int32)).astype(jnp.bfloat16)


def distances(depth):
    order = [depth // 2]
    for k in range(depth // 2 - 1, 0, -1):
        order += [k, -k]
    return order + [0]


def after(value, *others):
    return lax.optimization_barrier((value,) + others)[0]


def along_z(value, by):
    depth = lax.axis_size("z")
    return lax.ppermute(value, "z", [(i, (i + by) % depth) for i in range(depth)])


def split_kernel(level_ref, hidden_ref, *refs):
    outs, held = refs[:-1], refs[-1]
    depth, _, wide = held.shape
    share = wide // 2
    for z in range(depth):
        low = hidden_ref[:, z * share : (z + 1) * share]
        high = hidden_ref[:, (depth + z) * share : (depth + z + 1) * share]
        held[z] = jnp.concatenate([low, high], axis=1)
    for out, by in zip(outs, distances(depth)):
        out[...] = held[lax.rem(level_ref[0] + (by + depth), depth)]


def split_levels(hidden, level, depth):
    rows, width = hidden.shape
    block = (rows, width // depth)
    whole = pl.BlockSpec(memory_space=pltpu.VMEM)
    return pl.pallas_call(
        split_kernel,
        out_shape=[jax.ShapeDtypeStruct(block, hidden.dtype)] * depth,
        in_specs=[pl.BlockSpec(memory_space=pltpu.SMEM), whole],
        out_specs=[whole] * depth,
        scratch_shapes=[pltpu.VMEM((depth,) + block, hidden.dtype)],
        compiler_params=pltpu.CompilerParams(vmem_limit_bytes=40 << 20),
    )(level, hidden)


def join_kernel(level_ref, *refs):
    parts, out_ref, held = refs[:-2], refs[-2], refs[-1]
    depth, _, wide = held.shape
    share = wide // 2
    for part, by in zip(parts, distances(depth)):
        held[lax.rem(level_ref[0] + (by + depth), depth)] = part[...]
    for z in range(0, depth, 2):
        for s in range(2):
            pair = [held[z + i, :, s * share : (s + 1) * share] for i in range(2)]
            out_ref[:, (s * depth + z) * share : (s * depth + z + 2) * share] = (
                jnp.concatenate(pair, axis=1)
            )


def join_levels(parts, level):
    depth = len(parts)
    rows, wide = parts[0].shape
    whole = pl.BlockSpec(memory_space=pltpu.VMEM)
    return pl.pallas_call(
        join_kernel,
        out_shape=jax.ShapeDtypeStruct((rows, depth * wide), parts[0].dtype),
        in_specs=[pl.BlockSpec(memory_space=pltpu.SMEM)] + [whole] * depth,
        out_specs=whole,
        scratch_shapes=[pltpu.VMEM((depth, rows, wide), parts[0].dtype)],
        compiler_params=pltpu.CompilerParams(vmem_limit_bytes=40 << 20),
    )(level, *parts)


def halves_of(ref, core, half):
    own = pl.multiple_of(core * half, half)
    return ref[..., pl.ds(own, half)], ref[..., pl.ds(pl.multiple_of(half - own, half), half)]


def join_rows_kernel(place_ref, core_ref, next_ref, own_ref, mate_ref, own_scales, mate_scales, *refs):
    rows_refs, out_ref, passed_ref = refs[:-2], refs[-2], refs[-1]
    for i in range(next_ref.shape[0]):
        passed_ref[i] = next_ref[i]
    half = own_ref.shape[0]
    pairs = [halves_of(ref, core_ref[0], half) for ref in rows_refs]
    own = jnp.concatenate([pair[0][0] for pair in pairs])
    mate = jnp.concatenate([pair[1][0] for pair in pairs])
    total = own_scales[...] * jnp.dot(own, own_ref[...], preferred_element_type=jnp.float32)
    total += mate_scales[...] * jnp.dot(mate, mate_ref[...], preferred_element_type=jnp.float32)
    places, steps, slots, wide = out_ref.shape
    total = total.reshape(steps, places, slots, wide).astype(out_ref.dtype)
    for step in range(steps):
        out_ref[:, step] = total[step]


def join_rows(where, core, then, values, codes, scales, places):
    steps = where.shape[0]
    _, rows, cols = values.shape
    half, wide = codes[0].shape

    def rows_spec(j):
        return pl.BlockSpec((1, rows, cols), lambda i, w, c: (w[j], 0, 0))

    def whole(*shape):
        return pl.BlockSpec(shape, lambda i, w, c: (0,) * len(shape))

    words = pl.BlockSpec(memory_space=pltpu.SMEM)
    shape = (places, steps, rows // places, wide)
    return pl.pallas_call(
        join_rows_kernel,
        out_shape=[pltpu.HBM(shape, jnp.bfloat16), jax.ShapeDtypeStruct(then.shape, then.dtype)],
        grid_spec=pltpu.PrefetchScalarGridSpec(
            num_scalar_prefetch=2,
            grid=(1,),
            in_specs=[words] + [whole(half, wide)] * 2 + [whole(1, wide)] * 2
            + [rows_spec(j) for j in range(steps)],
            out_specs=[whole(*shape), words],
        ),
        compiler_params=pltpu.CompilerParams(vmem_limit_bytes=40 << 20),
    )(where, core, then, *codes, *scales, *[values] * steps)


def weight_kernel(core_ref, values_ref, mate_values_ref, own_ref, mate_ref, out_ref):
    half = out_ref.shape[1]
    own_rows = halves_of(values_ref, core_ref[0], half)[0].reshape(-1, half)
    mate_rows = halves_of(mate_values_ref, core_ref[0], half)[0].reshape(-1, half)
    part = lax.dot_general(
        jnp.concatenate([own_ref[...], mate_ref[...]]),
        jnp.concatenate([own_rows, mate_rows]),
        (((0,), (0,)), ((), ())),
        preferred_element_type=jnp.float32,
    )

    @pl.when(pl.program_id(0) == 0)
    def _():
        out_ref[...] = part

    @pl.when(pl.program_id(0) > 0)
    def _():
        out_ref[...] += part


def weight_sums(core, values, mate_values, own, mate, levels=2):
    depth, rows, cols = values.shape
    wide, half = own.shape[1], cols // 2
    units = pl.BlockSpec((levels * rows, wide), lambda i, c: (i, 0))
    return pl.pallas_call(
        weight_kernel,
        out_shape=pltpu.HBM((wide, half), jnp.float32),
        grid_spec=pltpu.PrefetchScalarGridSpec(
            num_scalar_prefetch=1,
            grid=(depth // levels,),
            in_specs=[
                pl.BlockSpec((levels, rows, cols), lambda i, c: (i, 0, 0)),
                pl.BlockSpec((levels, rows, cols), lambda i, c: (i, 0, 0)),
                units,
                units,
            ],
            out_specs=pl.BlockSpec((wide, half), lambda i, c: (0, 0)),
        ),
        compiler_params=pltpu.CompilerParams(vmem_limit_bytes=40 << 20),
    )(core, values, mate_values, own, mate)


def rows_kernel(counts_ref, rows_ref, out_ref):
    experts, slots, cols = out_ref.shape
    rows = rows_ref.shape[0]
    slot = lax.broadcasted_iota(jnp.int32, (slots, rows), 0)
    row = lax.broadcasted_iota(jnp.int32, (slots, rows), 1)
    hot, start = [], 0
    for e in range(experts):
        count = counts_ref[e]
        hit = jnp.logical_and(row == slot + start, slot < count)
        hot.append(jnp.where(hit, 1.0, 0.0))
        start = start + count
    hot = jnp.concatenate(hot).astype(jnp.bfloat16)
    packed = jnp.dot(hot, rows_ref[...], preferred_element_type=jnp.float32)
    out_ref[...] = packed.reshape(experts, slots, cols).astype(out_ref.dtype)


def pack_rows(counts, cotangent, slots):
    rows, cols = cotangent.shape
    whole = pl.BlockSpec(memory_space=pltpu.VMEM)
    return pl.pallas_call(
        rows_kernel,
        out_shape=jax.ShapeDtypeStruct((counts.shape[0], slots, cols), cotangent.dtype),
        in_specs=[pl.BlockSpec(memory_space=pltpu.SMEM), whole],
        out_specs=whole,
        compiler_params=pltpu.CompilerParams(vmem_limit_bytes=40 << 20),
    )(counts, cotangent)


def unpack_kernel(hot_ref, back_ref, *outs):
    experts, _, slots, wide = back_ref.shape
    for i, out in enumerate(outs):
        packed = back_ref[:, i].astype(jnp.float32).reshape(experts * slots, wide)
        out[...] = lax.dot_general(
            hot_ref[i], packed.astype(jnp.bfloat16), (((0,), (0,)), ((), ())),
            preferred_element_type=jnp.float32,
        ).astype(out.dtype)


def unpack(hot, back):
    steps, _, rows = hot.shape
    whole = pl.BlockSpec(memory_space=pltpu.VMEM)
    return pl.pallas_call(
        unpack_kernel,
        out_shape=[jax.ShapeDtypeStruct((rows, back.shape[-1]), back.dtype)] * steps,
        in_specs=[whole, whole],
        out_specs=[whole] * steps,
        compiler_params=pltpu.CompilerParams(vmem_limit_bytes=40 << 20),
    )(hot, back)


def pack_kernel(level_ref, hot_ref, *refs):
    blocks, out_ref = refs[:-1], refs[-1]
    experts, depth, slots, wide = out_ref.shape
    for i, by in enumerate(distances(depth)):
        packed = jnp.dot(hot_ref[i], blocks[i][...], preferred_element_type=jnp.float32)
        level = lax.rem(level_ref[0] + (by + depth), depth)
        out_ref[:, level] = packed.reshape(experts, slots, wide).astype(out_ref.dtype)


def pack_hidden(hot, blocks, level, experts):
    depth, places, rows = hot.shape
    wide = blocks[0].shape[1]
    whole = pl.BlockSpec(memory_space=pltpu.VMEM)
    return pl.pallas_call(
        pack_kernel,
        out_shape=pltpu.HBM((experts, depth, places // experts, wide), jnp.bfloat16),
        in_specs=[pl.BlockSpec(memory_space=pltpu.SMEM)] + [whole] * (depth + 1),
        out_specs=whole,
        compiler_params=pltpu.CompilerParams(vmem_limit_bytes=40 << 20),
    )(level, hot, *blocks)


def shards(cotangent, hidden, codes, scales, counts):
    rows, cols = cotangent.shape
    half = cols // 2
    share = codes.shape[1]
    places = lax.axis_size(PLACES)
    depth = lax.axis_size("z")
    experts = counts.shape[1]
    slots = 3 * rows // (2 * experts)
    wide = 2 * share
    order = distances(depth)
    place, core = lax.axis_index(PLACES), lax.axis_index("c")
    side, level = lax.axis_index("xl"), lax.axis_index("z")
    core_word = core.astype(jnp.int32).reshape(1)
    level_word = level.astype(jnp.int32).reshape(1)

    def levels_at(steps):
        return (level.astype(jnp.int32) + jnp.array(steps, jnp.int32) + depth) % depth

    line_at = ((place * 2 + core) * 2 + side) * depth
    own_counts = lax.dynamic_slice_in_dim(counts, line_at + level, 1, 0).reshape(experts)
    line_counts = lax.dynamic_slice_in_dim(counts, line_at, depth, 0)
    near_counts = lax.dynamic_slice_in_dim(jnp.concatenate([line_counts] * 2), level, depth, 0)
    near_counts = jnp.stack([near_counts[by % depth] for by in order])
    near_hot = slot_hot(near_counts, slots, rows).reshape(depth, experts * slots, rows)

    other_codes, other_scales = lax.ppermute((codes[0], scales[0]), "xl", SWAP)
    by_level = split_levels(hidden, level_word, depth)

    packed = pack_rows(own_counts, cotangent, slots)
    arrived = lax.all_to_all(packed, PLACES, 0, 0).reshape(places * slots, cols)

    line_hidden = {}
    for block, by in zip(by_level, order):
        line_hidden[-by if by < depth // 2 else by] = along_z(block, by) if by else block
    arrived, line_hidden[-1], line_hidden[1] = lax.optimization_barrier(
        (arrived, line_hidden[-1], line_hidden[1])
    )
    values = lax.all_gather(arrived, "z", axis=0, tiled=True)
    values = values.reshape(depth, places * slots, cols)

    other_codes, other_scales, *line_hidden = lax.optimization_barrier(
        [other_codes, other_scales] + [line_hidden[by] for by in order]
    )

    hidden_slots = pack_hidden(near_hot, line_hidden, level_word, experts)
    other_codes, other_scales = after((other_codes, other_scales), hidden_slots)
    first = side == 0
    both_codes = jnp.where(first, jnp.stack([codes[0], other_codes]),
                           jnp.stack([other_codes, codes[0]])).reshape(wide, half).T
    both_scales = jnp.where(first, jnp.stack([scales[0], other_scales]),
                            jnp.stack([other_scales, scales[0]])).reshape(1, wide)
    mate_scales, mate_codes = lax.ppermute((both_scales, both_codes), "c", SWAP)

    own_hidden = lax.all_to_all(hidden_slots, PLACES, 0, 0)
    own_hidden = own_hidden.transpose(1, 0, 2, 3).reshape(depth * places * slots, wide)
    mate_hidden = lax.ppermute(own_hidden, "c", SWAP)
    values, mate_codes, mate_scales = lax.optimization_barrier((values, mate_codes, mate_scales))
    values = after(values, own_hidden)
    gathered = values
    values = pltpu.with_memory_space_constraint(values, pltpu.HBM)

    def join(where, then):
        return join_rows(
            where, core_word, then, values, (both_codes, mate_codes), (both_scales, mate_scales), places
        )

    came = {}

    def send_home(steps, back):
        for by, block in zip(steps, back):
            came[-by if by < depth // 2 else by] = along_z(block, by) if by else block

    cut = 3
    far_at, close_at = levels_at(order[:cut]), levels_at(order[cut:])
    far_joined, close_at = join(far_at, close_at)
    close_joined, _ = join(close_at, far_at)
    mate_values = lax.ppermute(gathered, "c", SWAP)
    far_raw = after(lax.all_to_all(far_joined, PLACES, 0, 0), close_joined)
    far_back = unpack(near_hot[:cut], far_raw)
    send_home(order[:cut], far_back)
    own_hidden, mate_hidden = after((own_hidden, mate_hidden), *far_back)
    sums = weight_sums(core_word, values, mate_values, own_hidden, mate_hidden)
    sums = sums.reshape(2, share, half)
    gone = lax.dynamic_index_in_dim(sums, 1 - side, 0, keepdims=False)
    kept = lax.dynamic_index_in_dim(sums, side, 0, keepdims=False)
    largest = jnp.maximum(jnp.max(jnp.abs(gone)), 1e-30).reshape(1)
    gone = (gone * (1 / largest)).astype(jnp.float16)
    close_raw = after(lax.all_to_all(close_joined, PLACES, 0, 0), *came.values(), gone, kept)
    send_home(order[cut:], unpack(near_hot[cut:], close_raw))

    largest = lax.ppermute(largest, "xl", SWAP)
    gone, kept, largest, _ = lax.optimization_barrier((gone, kept, largest, close_raw))
    gone = lax.ppermute(gone, "xl", SWAP)
    weight_grad = kept + gone.astype(jnp.float32) * largest
    d_hidden = join_levels([came[by] for by in order], after(level_word, weight_grad))
    return d_hidden, weight_grad[None]


def solution(mesh):
    lanes, lines = mesh.devices.shape
    fine = Mesh(mesh.devices.reshape(2, lanes // 4, 2, 2, lines // 2), ("xh", "y", "c", "xl", "z"))
    expert, dp = ("xh", "y", "c"), ("xl", "z")
    in_specs = (P(expert + dp, None), P(expert + dp, None), P(expert, dp, None), P(expert, dp), P())
    out_specs = (P(expert + dp, None), P(expert, dp, None))
    return jax.shard_map(shards, mesh=fine, in_specs=in_specs, out_specs=out_specs, check_vma=False)
```
